32 devices in a mesh: gx: 8 (over z, x), gy: 4 (over y, core).
Axes of the slice: x: 2, y: 2, z: 4, core: 2. Of those that a mesh axis runs over, the one named last changes fastest.
Arguments:
- positions: float32 [8, 4, 3, 128], P('gx', 'gy'), may hold values from 0 to 29
- species: int32 [8, 4, 128], P('gx', 'gy'), may hold values from 0 to 4
- senders: int32 [8, 4, 3, 128], P('gx', 'gy'), may hold values from 0 to 639, as said below
- counts: int32 [8, 4, 128], P('gx', 'gy'), may hold values from 1 to 3, as said below
- owners: int32 [8, 4, 3, 128], P('gx', 'gy'), may hold values 0 or 1
- send_list: int32 [8, 4, 64], P('gx', 'gy'), may hold values from 0 to 127, as said below
- embedding: float32 [128, 5], replicated, may hold values from -6 to 6
- radial_in_one: float32 [64, 8], replicated, may hold values from -2 to 2
- radial_mid_one: float32 [64, 64], replicated, may hold values from -0.75 to 0.75
- radial_out_one: float32 [384, 64], replicated, may hold values from -0.75 to 0.75
- mixing: float32 [3, 128, 128], replicated, may hold values from -0.5 to 0.5
- square_mix: float32 [128, 128], replicated, may hold values from -0.5 to 0.5
- readout_one: float32 [128], replicated, may hold values from -0.5 to 0.5
- radial_in_two: float32 [64, 8], replicated, may hold values from -2 to 2
- radial_mid_two: float32 [64, 64], replicated, may hold values from -0.75 to 0.75
- radial_out_two: float32 [384, 64], replicated, may hold values from -0.75 to 0.75
- mix_two: float32 [128, 128], replicated, may hold values from -0.5 to 0.5
- read_hidden: float32 [16, 128], replicated, may hold values from -0.5 to 0.5
- read_out: float32 [16], replicated, may hold values from -1.5 to 1.5
Outputs:
- forces: float32 [8, 4, 3, 128], P('gx', 'gy')
- energies: float32 [8, 4, 128], P('gx', 'gy')
The draws below stay inside these ranges and needn't reach their ends.
Inputs may be any that keep to these rules, and one draw needn't show every extreme that they name: `counts`: every atom has at least one live slot, and some atom of every domain has all 3 slots live. `send_list`: each domain's list holds 64 distinct atoms of that domain. `senders`: an atom's slots name distinct atoms other than itself. Atom n of a domain sits at lattice site ((n // 2) // 8, (n // 2) % 8, n % 2); a ghost taken from the domain at offset (i - 1, j - 1) sits at its own site in that domain plus ((i - 1) * 8, (j - 1) * 8, 0). The site of every atom that a slot names differs from the site of the slot's atom by at most one along each of the three dimensions.
All inputs are finite; a program needn't handle non-finite values. No bound on the sum of `owners` on one device may be relied on, other than what follows from the above.
Results may differ from the reference program's by a relative error of at most 0.0003.
Values sent between devices are 32-bit elements; how exact they have to be, the bound alone decides.
A program may use at most 64 MiB of HBM per device.

```python
import math
import jax
import jax.numpy as jnp
from jax import lax

CH = 128
RADIAL = 64
NBASIS = 8
READ = 16
SPECIES = 5
NEIGH = 3
SIDE = 8
LAYERS = 2
ATOMS_DEV = 128
BOUND_DEV = 64
GRID_X = 8
GRID_Y = 4


def lattice_sites():
    atom_index = jnp.arange(SIDE * SIDE * LAYERS)
    column = atom_index // LAYERS
    return (column // SIDE, column % SIDE, atom_index % LAYERS, atom_index)


def ghost_plan(key):
    lattice_key = jax.random.fold_in(key, 7)
    score_key, order_key = jax.random.split(lattice_key)
    site_x, site_y, site_z, atom_index = lattice_sites()
    atoms = SIDE * SIDE * LAYERS
    domains = GRID_X * GRID_Y
    on_edge = ((site_x == 0) | (site_x == SIDE - 1) | (site_y == 0) | (site_y == SIDE - 1)).astype(jnp.int32)
    noise_bits = jax.random.randint(score_key, (domains, atoms), 0, 1 << 16)
    scores = (noise_bits + on_edge[None, :] * (1 << 16)) * atoms + atom_index[None, :]
    top_values, chosen = lax.top_k(scores, BOUND_DEV)
    order_keys = jax.random.split(order_key, domains)
    shuffled = jax.vmap(lambda single, picked: picked[jax.random.permutation(single, BOUND_DEV)])(order_keys, chosen)
    inverse = jax.vmap(lambda picked: jnp.zeros((atoms,), jnp.int32).at[picked].set(jnp.arange(BOUND_DEV).astype(jnp.int32)))(shuffled)
    return (shuffled.astype(jnp.int32), inverse)


def draw_send_list(key, part):
    shuffled, inverse = ghost_plan(key)
    return shuffled.reshape(GRID_X, GRID_Y, BOUND_DEV).astype(jnp.int32)


def draw_senders(key, part):
    shuffled, inverse = ghost_plan(key)
    site_x, site_y, site_z, atom_index = lattice_sites()
    atoms = SIDE * SIDE * LAYERS
    domains = GRID_X * GRID_Y
    offsets = jnp.arange(27)
    step_x = offsets // 9 - 1
    step_y = offsets // 3 % 3 - 1
    step_z = offsets % 3 - 1
    target_z = site_z[:, None] + step_z[None, :]
    usable = (target_z >= 0) & (target_z < LAYERS) & (offsets[None, :] != 13)
    noise_bits = jax.random.randint(jax.random.fold_in(key, 13), (domains, atoms, 27), 0, 1 << 16)
    scores = jnp.where(usable[None], noise_bits * 32 + offsets[None, None, :], -1)
    top_values, picked = lax.top_k(scores, NEIGH)
    target_x = site_x[None, :, None] + step_x[picked]
    target_y = site_y[None, :, None] + step_y[picked]
    target_layer = site_z[None, :, None] + step_z[picked]
    block_x = (target_x >= 0).astype(jnp.int32) + (target_x >= SIDE).astype(jnp.int32)
    block_y = (target_y >= 0).astype(jnp.int32) + (target_y >= SIDE).astype(jnp.int32)
    wrapped = (target_x % SIDE * SIDE + target_y % SIDE) * LAYERS + target_layer
    domain_ids = jnp.arange(domains)
    first_at = (domain_ids // GRID_Y)[:, None, None]
    second_at = (domain_ids % GRID_Y)[:, None, None]
    owner_domain = (first_at + block_x - 1) % GRID_X * GRID_Y + (second_at + block_y - 1) % GRID_Y
    slot_place = inverse[owner_domain, wrapped]
    block_id = 3 * block_x + block_y
    compact = block_id - (block_id > 4).astype(jnp.int32)
    ghost_index = atoms + compact * BOUND_DEV + slot_place
    sender = jnp.where(block_id == 4, wrapped, ghost_index)
    return jnp.moveaxis(sender.reshape(GRID_X, GRID_Y, atoms, NEIGH), 3, 2).astype(jnp.int32)


def draw_positions(key, part):
    site_x, site_y, site_z, atom_index = lattice_sites()
    atoms = SIDE * SIDE * LAYERS
    lattice = jnp.stack([(site_x.astype(jnp.float32) + 0.5) * 1.75, (site_y.astype(jnp.float32) + 0.5) * 1.75, (site_z.astype(jnp.float32) + 0.5) * 3.25])
    widths = jnp.array([1.75, 1.75, 3.25], jnp.float32)[:, None]
    jitter_key = jax.random.fold_in(key, 5)
    jitter = jax.random.uniform(jitter_key, (GRID_X, GRID_Y, 3, atoms), minval=-0.25, maxval=0.25)
    return (lattice[None, None] + jitter * widths[None, None]).astype(jnp.float32)


def draw_counts(key, part):
    count_key = jax.random.fold_in(key, 11)
    dense_key, bits_key, pick_key = jax.random.split(count_key, 3)
    dense_flag = jax.random.randint(dense_key, (GRID_X, GRID_Y, 1), 0, 2)
    lowest = jnp.where(dense_flag == 1, NEIGH // 2, 1)
    lowest = jnp.maximum(lowest, 1)
    raw_bits = jax.random.randint(bits_key, (GRID_X, GRID_Y, ATOMS_DEV), 0, 1 << 20)
    counts = lowest + raw_bits % (NEIGH + 1 - lowest)
    chosen = jax.random.randint(pick_key, (GRID_X, GRID_Y, 1), 0, ATOMS_DEV)
    atom_iota = jnp.arange(ATOMS_DEV)[None, None, :]
    return jnp.where(atom_iota == chosen, NEIGH, counts).astype(jnp.int32)


def with_ends(values, own_key, least, largest):
    index_at = [jax.random.randint(jax.random.fold_in(own_key, axis), (), 0, length) for axis, length in enumerate(values.shape)]
    main_axis = values.shape.index(max(values.shape))
    next_to = index_at[:main_axis] + [(index_at[main_axis] + 1) % values.shape[main_axis]] + index_at[main_axis + 1:]
    return values.at[tuple(index_at)].set(least).at[tuple(next_to)].set(largest)


def centred(rng, shape, scale, limit, dtype=jnp.bfloat16):
    values = jax.random.normal(rng, shape, jnp.float32) * scale
    return jnp.minimum(jnp.maximum(values, -limit), limit).astype(dtype)


def setup_inputs(seed: int = 0) -> dict:
    key_of = jax.random.split(jax.random.key(seed), 20)
    return {
        "positions": draw_positions(jax.random.fold_in(key_of[19], 71), 0),
        "species": with_ends(jax.random.randint(key_of[1], (GRID_X, GRID_Y, ATOMS_DEV), 0, SPECIES), jax.random.fold_in(key_of[1], 1), 0, SPECIES - 1).astype(jnp.int32),
        "senders": draw_senders(jax.random.fold_in(key_of[19], 71), 0),
        "counts": draw_counts(jax.random.fold_in(key_of[19], 71), 0),
        "owners": with_ends((jax.random.randint(key_of[4], (GRID_X, GRID_Y, NEIGH, ATOMS_DEV), 0, 2) < 1).astype(jnp.int32), jax.random.fold_in(key_of[4], 1), 0, 1),
        "send_list": draw_send_list(jax.random.fold_in(key_of[19], 71), 0),
        "embedding": centred(key_of[6], (CH, SPECIES), 1.0, 6.0, jnp.float32),
        "radial_in_one": centred(key_of[7], (RADIAL, NBASIS), NBASIS ** -0.5, 2.0, jnp.float32),
        "radial_mid_one": centred(key_of[8], (RADIAL, RADIAL), RADIAL ** -0.5, 0.75, jnp.float32),
        "radial_out_one": centred(key_of[9], (3 * CH, RADIAL), RADIAL ** -0.5, 0.75, jnp.float32),
        "mixing": centred(key_of[10], (3, CH, CH), CH ** -0.5, 0.5, jnp.float32),
        "square_mix": centred(key_of[11], (CH, CH), CH ** -0.5, 0.5, jnp.float32),
        "readout_one": centred(key_of[12], (CH,), CH ** -0.5, 0.5, jnp.float32),
        "radial_in_two": centred(key_of[13], (RADIAL, NBASIS), NBASIS ** -0.5, 2.0, jnp.float32),
        "radial_mid_two": centred(key_of[14], (RADIAL, RADIAL), RADIAL ** -0.5, 0.75, jnp.float32),
        "radial_out_two": centred(key_of[15], (3 * CH, RADIAL), RADIAL ** -0.5, 0.75, jnp.float32),
        "mix_two": centred(key_of[16], (CH, CH), CH ** -0.5, 0.5, jnp.float32),
        "read_hidden": centred(key_of[17], (READ, CH), CH ** -0.5, 0.5, jnp.float32),
        "read_out": centred(key_of[18], (READ,), READ ** -0.5, 1.5, jnp.float32),
    }


precise = lax.Precision.HIGHEST
spacing = 1.75
cutoff = 5.0
soften = 0.25
pair_strength = 2.0

def product(left_side, right_side):
    return jnp.dot(left_side, right_side, precision=precise, preferred_element_type=jnp.float32)

def harmonics(direction):
    along_x = direction[0]
    along_y = direction[1]
    along_z = direction[2]
    root_three = math.sqrt(3.0)
    root_five = math.sqrt(5.0)
    root_fifteen = math.sqrt(15.0)
    return jnp.stack([jnp.ones_like(along_x), root_three * along_x, root_three * along_y, root_three * along_z, root_fifteen * along_x * along_y, root_fifteen * along_y * along_z, 0.5 * root_five * (2.0 * along_z * along_z - along_x * along_x - along_y * along_y), root_fifteen * along_x * along_z, 0.5 * root_fifteen * (along_x * along_x - along_y * along_y)])

def geometry(places, ghost_places, table_index, basis_count):
    places_all = jnp.concatenate([places, ghost_places], axis=1)
    repeats = table_index.shape[0] // places.shape[1]
    displace = places_all[:, table_index] - jnp.tile(places, (1, repeats))
    radius = jnp.sqrt(lax.optimization_barrier(jnp.sum(displace * displace, axis=0)) + soften)
    direction = displace / radius
    scaled_radius = jnp.minimum(radius / cutoff, 1.0)
    envelope = 1.0 - 28.0 * scaled_radius ** 6 + 48.0 * scaled_radius ** 7 - 21.0 * scaled_radius ** 8
    orders = jnp.arange(1, basis_count + 1).astype(jnp.float32)[:, None]
    radial_basis = math.sqrt(2.0 / cutoff) * jnp.sin(orders * math.pi * scaled_radius) / radius * envelope
    return (harmonics(direction), radial_basis, envelope, radius)

def radial(radial_basis, weight_in, weight_mid, weight_out):
    hidden = jax.nn.silu(product(weight_in, radial_basis))
    hidden = jax.nn.silu(product(weight_mid, hidden))
    return product(weight_out, hidden)

def flat_index(senders, atom_count, bound_count):
    ghost_slot = senders - atom_count
    blocks_of = ghost_slot // bound_count
    blocks_of = blocks_of + (blocks_of >= 4).astype(jnp.int32)
    spot = atom_count + blocks_of * bound_count + ghost_slot % bound_count
    return jnp.where(senders < atom_count, senders, spot).reshape(-1).astype(jnp.int32)

def live_slots(counts, slot_count):
    return (jnp.arange(slot_count)[:, None] < counts[None, :]).astype(jnp.float32).reshape(-1)

def ghost_shift(bound_count):
    blocks_of = jnp.arange(9 * bound_count) // bound_count
    side_length = spacing * SIDE
    shift_x = (blocks_of // 3 - 1).astype(jnp.float32) * side_length
    shift_y = (blocks_of % 3 - 1).astype(jnp.float32) * side_length
    return jnp.stack([shift_x, shift_y, jnp.zeros_like(shift_x)])

def layer_one(places, ghost_places, embedded, ghost_embedded, table_index, live_mask, owner_mask, weight_in, weight_mid, weight_out, mixing, square_mix, readout_one):
    shapes, radial_basis, envelope, radius = geometry(places, ghost_places, table_index, weight_in.shape[1])
    atom_count = places.shape[1]
    channels = embedded.shape[0]
    slot_count = table_index.shape[0] // atom_count
    edge_weight = radial(radial_basis, weight_in, weight_mid, weight_out).reshape(3, channels, -1)
    sender_rows = jnp.concatenate([embedded, ghost_embedded], axis=1)[:, table_index]
    carried = (edge_weight * (sender_rows * live_mask)[None]).reshape(3, channels, slot_count, atom_count)
    shaped = shapes.reshape(9, slot_count, atom_count)
    scalar_part = jnp.einsum('cna,na->ca', carried[0], shaped[0], precision=precise)[None]
    vector_part = jnp.einsum('cna,kna->kca', carried[1], shaped[1:4], precision=precise)
    tensor_part = jnp.einsum('cna,kna->kca', carried[2], shaped[4:9], precision=precise)
    moments = jnp.concatenate([scalar_part, vector_part, tensor_part], 0) / slot_count
    squares = lax.optimization_barrier(jnp.sum(moments * moments, axis=0))
    scalar_feature = product(mixing[0], moments[0]) + product(square_mix, squares) + embedded
    vectors = jnp.einsum('ij,kja->kia', mixing[1], moments[1:4], precision=precise)
    tensors = jnp.einsum('ij,kja->kia', mixing[2], moments[4:9], precision=precise)
    features = jnp.concatenate([scalar_feature[None], vectors, tensors], 0).reshape(9 * channels, atom_count)
    pair_energy = (owner_mask * live_mask * pair_strength * jnp.exp(-radius) * envelope).reshape(slot_count, atom_count).sum(0)
    energy = product(readout_one, scalar_feature) + pair_energy
    return (features, energy)

def layer_two(places, ghost_places, features, ghost_features, table_index, live_mask, weight_in, weight_mid, weight_out, mix_two, read_hidden, read_out):
    shapes, radial_basis, envelope, radius = geometry(places, ghost_places, table_index, weight_in.shape[1])
    atom_count = places.shape[1]
    channels = mix_two.shape[0]
    slot_count = table_index.shape[0] // atom_count
    edge_weight = radial(radial_basis, weight_in, weight_mid, weight_out).reshape(3, channels, -1)
    sender_rows = jnp.concatenate([features, ghost_features], axis=1)[:, table_index].reshape(9, channels, -1)
    projected = sender_rows * shapes[:, None, :]
    scalar = (edge_weight[0] * projected[0] + edge_weight[1] * lax.optimization_barrier(jnp.sum(projected[1:4], 0)) + edge_weight[2] * lax.optimization_barrier(jnp.sum(projected[4:9], 0))) * live_mask
    gathered = scalar.reshape(channels, slot_count, atom_count).sum(1) / slot_count
    refined = product(mix_two, gathered) + features[:channels]
    return product(read_out, jax.nn.silu(product(read_hidden, refined)))

def reference(positions, species, senders, counts, owners, send_list, embedding, radial_in_one, radial_mid_one, radial_out_one, mixing, square_mix, readout_one, radial_in_two, radial_mid_two, radial_out_two, mix_two, read_hidden, read_out):
    grid_x = positions.shape[0]
    grid_y = positions.shape[1]
    atom_count = positions.shape[3]
    bound_count = send_list.shape[2]
    slot_count = senders.shape[2]
    domains = grid_x * grid_y
    embedded_all = jnp.moveaxis(embedding[:, species], 0, 2)
    picker = send_list[:, :, None, :]
    bound_places = jnp.take_along_axis(positions, picker, axis=3)
    bound_embedded = jnp.take_along_axis(embedded_all, picker, axis=3)
    offsets = ghost_shift(bound_count)
    domain_ids = jnp.arange(domains).astype(jnp.int32)

    def beside_all(table, first_at, second_at):
        pieces = [table[(first_at + step_x - 1) % grid_x, (second_at + step_y - 1) % grid_y] for step_x in range(3) for step_y in range(3)]
        stacked = jnp.stack(pieces, 1)
        return stacked.reshape(stacked.shape[0], -1)

    def deposit(buffer, returned, first_at, second_at):
        pieces = returned.reshape(returned.shape[0], 9, bound_count)
        for step_x in range(3):
            for step_y in range(3):
                buffer = buffer.at[(first_at + step_x - 1) % grid_x, (second_at + step_y - 1) % grid_y].add(pieces[:, 3 * step_x + step_y])
        return buffer

    def unpack(domain):
        first_at = domain // grid_y
        second_at = domain % grid_y
        table_index = flat_index(senders[first_at, second_at], atom_count, bound_count)
        live_mask = live_slots(counts[first_at, second_at], slot_count)
        owner_mask = owners[first_at, second_at].astype(jnp.float32).reshape(-1)
        ghost_places = beside_all(bound_places, first_at, second_at) + offsets
        ghost_embedded = beside_all(bound_embedded, first_at, second_at)
        return (first_at, second_at, table_index, live_mask, owner_mask, ghost_places, ghost_embedded)

    def first_pass(domain):
        first_at, second_at, table_index, live_mask, owner_mask, ghost_places, ghost_embedded = unpack(domain)
        return layer_one(positions[first_at, second_at], ghost_places, embedded_all[first_at, second_at], ghost_embedded, table_index, live_mask, owner_mask, radial_in_one, radial_mid_one, radial_out_one, mixing, square_mix, readout_one)
    features_flat, energy_one = lax.map(first_pass, domain_ids)
    features_all = features_flat.reshape(grid_x, grid_y, -1, atom_count)
    feature_rows = features_all.shape[2]
    bound_features = jnp.take_along_axis(features_all, picker, axis=3)

    def second_pass(buffer, domain):
        first_at, second_at, table_index, live_mask, owner_mask, ghost_places, ghost_embedded = unpack(domain)
        ghost_features = beside_all(bound_features, first_at, second_at)

        def second_layer(place_arg, ghost_arg, feature_arg, ghost_feature_arg):
            return layer_two(place_arg, ghost_arg, feature_arg, ghost_feature_arg, table_index, live_mask, radial_in_two, radial_mid_two, radial_out_two, mix_two, read_hidden, read_out)
        energy_two, pullback = jax.vjp(second_layer, positions[first_at, second_at], ghost_places, features_all[first_at, second_at], ghost_features)
        grad_places, grad_ghosts, grad_features, grad_ghost_features = pullback(jnp.ones_like(energy_two))
        returned = jnp.concatenate([grad_ghost_features, grad_ghosts], 0)
        buffer = deposit(buffer, returned, first_at, second_at)
        return (buffer, (energy_two, grad_places, grad_features))
    buffer = jnp.zeros((grid_x, grid_y, feature_rows + 3, bound_count), jnp.float32)
    buffer, (energy_two, grad_places_two, grad_features_all) = lax.scan(second_pass, buffer, domain_ids)

    def third_pass(domain):
        first_at, second_at, table_index, live_mask, owner_mask, ghost_places, ghost_embedded = unpack(domain)
        back_rows = buffer[first_at, second_at]
        grad_features = grad_features_all[domain].at[:, send_list[first_at, second_at]].add(back_rows[:feature_rows])

        def first_layer(place_arg, ghost_arg):
            return layer_one(place_arg, ghost_arg, embedded_all[first_at, second_at], ghost_embedded, table_index, live_mask, owner_mask, radial_in_one, radial_mid_one, radial_out_one, mixing, square_mix, readout_one)
        outputs, pullback = jax.vjp(first_layer, positions[first_at, second_at], ghost_places)
        return pullback((grad_features, jnp.ones((atom_count,), jnp.float32)))
    grad_first, grad_ghost_first = lax.map(third_pass, domain_ids)

    def fourth_pass(place_buffer, domain):
        return (deposit(place_buffer, grad_ghost_first[domain], domain // grid_y, domain % grid_y), domain)
    place_buffer = jnp.zeros((grid_x, grid_y, 3, bound_count), jnp.float32)
    place_buffer, unused = lax.scan(fourth_pass, place_buffer, domain_ids)
    grad_total = (grad_first + grad_places_two).reshape(grid_x, grid_y, 3, atom_count)
    back_places = buffer[:, :, feature_rows:] + place_buffer

    def settle(grad_domain, back_domain, pick_rows):
        return grad_domain.at[:, pick_rows].add(back_domain)
    grad_total = jax.vmap(jax.vmap(settle))(grad_total, back_places, send_list)
    energies = (energy_one + energy_two).reshape(grid_x, grid_y, atom_count)
    return (-grad_total, energies)
```

```python
import functools
import math

import jax
import jax.numpy as jnp
from jax import lax
from jax.experimental import pallas as pl
from jax.experimental.pallas import tpu as pltpu
from jax.sharding import PartitionSpec as P

SIDE = 8
SPACING = 1.75
CUTOFF = 5.0
SOFTEN = 0.25
PAIR = 2.0
ROWS = 16
DEGREE = (0, 1, 1, 1, 2, 2, 2, 2, 2)
MEMBERS = ((0,), (1, 2, 3), (4, 5, 6, 7, 8))
F32 = jnp.float32
BF16 = jnp.bfloat16
NN = (((1,), (0,)), ((), ()))
TN = (((0,), (0,)), ((), ()))
NT = (((1,), (1,)), ((), ()))


def dot(a, b, dims=NN):
    return lax.dot_general(a, b, dims, preferred_element_type=F32)


def split(x):
    high = x.astype(BF16)
    return high, (x - high.astype(F32)).astype(BF16)


def split_three(x):
    high = x.astype(BF16)
    rest = x - high.astype(F32)
    return (high,) + split(rest)


def mm(a, b, dims=NN):
    return dot(a[0], b[0], dims) + (dot(a[0], b[1], dims) + dot(a[1], b[0], dims))


def pick(parts, one_hot, dims=NN):
    out = dot(parts[-1], one_hot, dims)
    for part in parts[-2::-1]:
        out = out + dot(part, one_hot, dims)
    return out


def floor_div(x, by):
    return jnp.floor((x + 0.5) * (1.0 / by))


def one_hot_rows(index, rows):
    ids = lax.broadcasted_iota(jnp.int32, (rows, index.shape[1]), 0).astype(F32)
    return jnp.where(ids == index, 1.0, 0.0).astype(BF16)


def by_domain(stacked, domain, rows):
    out = jnp.where(domain == 0.0, stacked[:rows], 0.0)
    for d in range(1, 9):
        out = out + jnp.where(domain == float(d), stacked[d * rows : (d + 1) * rows], 0.0)
    return out


def silu_pair(h):
    gate = jax.nn.sigmoid(h)
    return h * gate, gate * (1.0 + h * (1.0 - gate))


def radial(basis, w_in, w_mid, w_out):
    s1, g1 = silu_pair(mm(w_in, split(basis)))
    s2, g2 = silu_pair(mm(w_mid, split(s1)))
    return mm(w_out, split(s2)), g1, g2


def radial_back(g_out, w_in, w_mid, w_out, g1, g2):
    gh2 = mm(w_out, split(g_out), TN) * g2
    gh1 = mm(w_mid, split(gh2), TN) * g1
    return mm(w_in, split(gh1), TN)


def kernel(
    layers,
    pos_ref, spec_ref, send_ref, cnt_ref, own_ref, list_ref, emb_ref,
    wi1_ref, wm1_ref, wo1_ref, mix_ref, sqm_ref, ro1_ref,
    wi2_ref, wm2_ref, wo2_ref, mx2_ref, rh_ref, ro2_ref,
    force_ref, energy_ref,
    table, grads, back, send_a, recv_a, send_b, recv_b,
):
    atoms = pos_ref.shape[3]
    bound = list_ref.shape[2]
    slots = send_ref.shape[2]
    channels = emb_ref.shape[0]
    species = emb_ref.shape[1]
    nbasis = wi1_ref.shape[1]
    column = SIDE * layers
    wide = 2 * atoms
    ring = (SIDE + 2) * layers
    used = (SIDE + 2) * ring
    me_x, me_y = lax.axis_index("gx"), lax.axis_index("gy")
    nx, ny = lax.axis_size("gx"), lax.axis_size("gy")

    def neighbour(d):
        return (lax.rem(me_x + (d // 3 - 1) + nx, nx), lax.rem(me_y + (d % 3 - 1) + ny, ny))

    others = [d for d in range(9) if d != 4]
    barrier = pltpu.get_barrier_semaphore()
    for d in others:
        pl.semaphore_signal(barrier, inc=1, device_id=neighbour(d), device_id_type=pl.DeviceIdType.MESH)

    table[4] = jnp.zeros((ROWS, atoms), F32)
    table[4, 0:3, :] = pos_ref[0, 0]
    table[4, 3:4, :] = spec_ref[0].astype(F32)
    table[4, 4 : 4 + slots, :] = send_ref[0, 0].astype(F32)
    table[4, 7:8, :] = cnt_ref[0].astype(F32)
    table[4, 8:9, 0:bound] = list_ref[0].astype(F32)
    pl.semaphore_wait(barrier, 8)
    copies = []
    for d in others:
        copy = pltpu.make_async_remote_copy(
            src_ref=table.at[4],
            dst_ref=table.at[8 - d],
            send_sem=send_a.at[d],
            recv_sem=recv_a.at[8 - d],
            device_id=neighbour(d),
            device_id_type=pl.DeviceIdType.MESH,
        )
        copy.start()
        copies.append(copy)

    lane = lax.broadcasted_iota(jnp.int32, (1, wide), 1).astype(F32)
    ring_at = lane - atoms
    low_x = ring_at < ring
    long_side = ring_at < 2 * ring
    along = jnp.where(low_x, ring_at, ring_at - ring)
    in_y = ring_at - 2 * ring
    low_y = in_y < column
    across = jnp.where(low_y, in_y, in_y - column)
    half_long = floor_div(along, layers)
    half_short = floor_div(across, layers)
    site_x = jnp.where(long_side, jnp.where(low_x, -1.0, float(SIDE)), half_short)
    site_y = jnp.where(long_side, half_long - 1.0, jnp.where(low_y, -1.0, float(SIDE)))
    site_z = jnp.where(long_side, along - half_long * layers, across - half_short * layers)
    inside = (lane < atoms) | (lane >= used)
    off_x = jnp.where(inside, 0.0, floor_div(site_x, SIDE))
    off_y = jnp.where(inside, 0.0, floor_div(site_y, SIDE))
    ring_atom = (site_x - off_x * SIDE) * column + (site_y - off_y * SIDE) * layers + site_z
    atom_r = jnp.where(lane < atoms, lane, jnp.where(lane >= used, 0.0, ring_atom))
    domain_r = 3.0 * (off_x + 1.0) + (off_y + 1.0)
    hot_r = one_hot_rows(atom_r, atoms)

    wi1, wm1, wo1 = split(wi1_ref[...]), split(wm1_ref[...]), split(wo1_ref[...])
    wi2, wm2, wo2 = split(wi2_ref[...]), split(wm2_ref[...]), split(wo2_ref[...])
    mix = [split(mix_ref[l]) for l in range(3)]
    sqm, mx2, rh = split(sqm_ref[...]), split(mx2_ref[...]), split(rh_ref[...])
    emb = split_three(emb_ref[...])
    ro1_cols = jnp.broadcast_to(ro1_ref[...], (atoms, channels)).T
    ro2_cols = jnp.broadcast_to(ro2_ref[...], (atoms, ro2_ref.shape[1])).T

    for copy in copies:
        copy.wait()

    def tile(x):
        return jnp.concatenate([x] * slots, axis=1)

    def slot(x, k):
        return x[:, k * wide : (k + 1) * wide]

    def own(x):
        return jnp.concatenate([x[:, k * wide : k * wide + atoms] for k in range(slots)], axis=1)

    def own_slot(x, k):
        return x[:, k * atoms : (k + 1) * atoms]

    def spread(x):
        zero = jnp.zeros((x.shape[0], atoms), F32)
        return jnp.concatenate([p for k in range(slots) for p in (own_slot(x, k), zero)], axis=1)

    everything = table[...].reshape(9 * ROWS, atoms)
    parts = split_three(everything)
    rec = by_domain(pick(parts, hot_r), domain_r, ROWS)
    sender = jnp.concatenate([rec[4 + k : 5 + k] for k in range(slots)], axis=1)
    live = jnp.concatenate(
        [jnp.where((rec[7:8] > float(k)) & (lane < used), 1.0, 0.0) for k in range(slots)], axis=1
    )
    is_local = sender < atoms
    ghost = sender - atoms
    block = floor_div(ghost, bound)
    place = ghost - block * bound
    block = jnp.where(block >= 4.0, block + 1.0, block)
    block = jnp.where(is_local, 4.0, block)
    block_x = floor_div(block, 3)
    block_y = block - 3.0 * block_x - 1.0
    block_x = block_x - 1.0
    to_x = tile(off_x) + block_x
    to_y = tile(off_y) + block_y
    domain_s = 3.0 * (to_x + 1.0) + (to_y + 1.0)
    lists = dot(parts[0], one_hot_rows(place, atoms))
    listed = jnp.zeros_like(sender)
    for d in range(9):
        listed = listed + jnp.where(domain_s == float(d), lists[d * ROWS + 8 : d * ROWS + 9], 0.0)
    atom_s = jnp.where(is_local, sender, listed)
    hot_s = one_hot_rows(atom_s, atoms)
    upper = jnp.concatenate([table[d, 0:8, :] for d in range(9)], axis=0)
    snd = by_domain(pick(split_three(upper), hot_s), domain_s, 8)

    side_length = SPACING * SIDE
    dx = (snd[0:1] + block_x * side_length) - tile(rec[0:1])
    dy = (snd[1:2] + block_y * side_length) - tile(rec[1:2])
    dz = snd[2:3] - tile(rec[2:3])
    radius = jnp.sqrt(dx * dx + dy * dy + dz * dz + SOFTEN)
    inverse = 1.0 / radius
    ux, uy, uz = dx * inverse, dy * inverse, dz * inverse
    x = jnp.minimum(radius / CUTOFF, 1.0)
    x2 = x * x
    x5 = x2 * x2 * x
    x6 = x5 * x
    envelope = 1.0 + x6 * (-28.0 + x * (48.0 - 21.0 * x))
    slope = jnp.where(radius < CUTOFF, 1.0 / CUTOFF, 0.0)
    d_envelope = x5 * (-168.0 + x * (336.0 - 168.0 * x)) * slope
    orders = (lax.broadcasted_iota(jnp.int32, (nbasis, 1), 0) + 1).astype(F32) * math.pi
    angle = orders * x
    scale = math.sqrt(2.0 / CUTOFF)
    sines = jnp.sin(angle) * scale
    cosines = jnp.cos(angle) * scale
    basis = sines * (inverse * envelope)
    d_basis = cosines * orders * (slope * inverse * envelope) + sines * (
        inverse * d_envelope - inverse * inverse * envelope
    )
    r3, r5, r15 = math.sqrt(3.0), math.sqrt(5.0), math.sqrt(15.0)
    shapes = [
        None,
        r3 * ux,
        r3 * uy,
        r3 * uz,
        r15 * ux * uy,
        r15 * uy * uz,
        0.5 * r5 * (2.0 * uz * uz - ux * ux - uy * uy),
        r15 * ux * uz,
        0.5 * r15 * (ux * ux - uy * uy),
    ]

    def rows_of(w, l):
        return w[l * channels : (l + 1) * channels]

    species_row = lax.broadcasted_iota(jnp.int32, (species, 1), 0).astype(F32)
    hot_es = jnp.where(species_row == snd[3:4], 1.0, 0.0).astype(BF16)
    hot_er = jnp.where(species_row == rec[3:4], 1.0, 0.0).astype(BF16)
    carrier = pick(emb, hot_es) * (live * (1.0 / slots))
    embedded = pick(emb, hot_er)
    edge_one, one_g1, one_g2 = radial(basis, wi1, wm1, wo1)
    carried = [rows_of(edge_one, l) * carrier for l in range(3)]
    moments = []
    for m in range(9):
        term = carried[DEGREE[m]] if m == 0 else carried[DEGREE[m]] * shapes[m]
        total = slot(term, 0)
        for k in range(1, slots):
            total = total + slot(term, k)
        moments.append(total)
    squares = moments[0] * moments[0]
    for m in range(1, 9):
        squares = squares + moments[m] * moments[m]
    features = [mm(mix[0], split(moments[0])) + mm(sqm, split(squares)) + embedded]
    for l in (1, 2):
        mixed = mm(mix[l], split(jnp.concatenate([moments[m] for m in MEMBERS[l]], axis=1)))
        features += [mixed[:, i * wide : (i + 1) * wide] for i in range(len(MEMBERS[l]))]

    live_two = own(live) * (1.0 / slots)
    edge_two, two_g1, two_g2 = radial(own(basis), wi2, wm2, wo2)
    shapes_two = [None] + [own(s) for s in shapes[1:]]
    at_two, to_x2, to_y2 = own(atom_s), own(to_x), own(to_y)
    ax = floor_div(at_two, column)
    rest = at_two - ax * column
    ay = floor_div(rest, layers)
    az = rest - ay * layers
    sx = ax + to_x2 * SIDE
    sy = ay + to_y2 * SIDE
    outside = jnp.where(
        to_x2 != 0.0,
        jnp.where(to_x2 < 0.0, 0.0, float(ring)) + (sy + 1.0) * layers + az,
        2.0 * ring + jnp.where(to_y2 < 0.0, 0.0, float(column)) + sx * layers + az,
    )
    at_ring = jnp.where((to_x2 == 0.0) & (to_y2 == 0.0), at_two, atoms + outside)
    hot_two = one_hot_rows(at_ring, wide)
    stacked = jnp.concatenate(features, axis=0)
    sent = pick(split(stacked), hot_two)
    projected = []
    for l in range(3):
        total = None
        for m in MEMBERS[l]:
            term = rows_of(sent, m) if m == 0 else rows_of(sent, m) * shapes_two[m]
            total = term if total is None else total + term
        projected.append(total)
    scalar = sum(rows_of(edge_two, l) * projected[l] for l in range(3)) * live_two
    gathered = own_slot(scalar, 0)
    for k in range(1, slots):
        gathered = gathered + own_slot(scalar, k)
    refined = mm(mx2, split(gathered)) + features[0][:, :atoms]
    hidden, hidden_slope = silu_pair(mm(rh, split(refined)))
    energy_two = jnp.sum(ro2_cols * hidden, axis=0, keepdims=True)
    energy_one = jnp.sum(ro1_cols * features[0][:, :atoms], axis=0, keepdims=True)
    owners = jnp.concatenate([own_ref[0, 0, k : k + 1, :].astype(F32) for k in range(slots)], axis=1)
    decay = PAIR * jnp.exp(-own(radius)) * owners * own(live)
    pair = decay * own(envelope)
    energy = energy_one + energy_two
    for k in range(slots):
        energy = energy + own_slot(pair, k)
    energy_ref[0] = energy
    g_radius_pair = decay * (own(d_envelope) - own(envelope))

    g_refined = mm(rh, split(ro2_cols * hidden_slope), TN)
    g_gathered = mm(mx2, split(g_refined), TN)
    t = jnp.concatenate([g_gathered] * slots, axis=1) * live_two
    g_edge_two = jnp.concatenate([t * projected[l] for l in range(3)], axis=0)
    g_proj = [t * rows_of(edge_two, l) for l in range(3)]
    g_sent = jnp.concatenate(
        [g_proj[0]] + [g_proj[DEGREE[m]] * shapes_two[m] for m in range(1, 9)], axis=0
    )
    g_shapes_two = [
        jnp.sum(g_proj[DEGREE[m]] * rows_of(sent, m), axis=0, keepdims=True) for m in range(1, 9)
    ]
    g_basis_two = radial_back(g_edge_two, wi2, wm2, wo2, two_g1, two_g2)
    g_stacked = pick(split(g_sent), hot_two, NT)
    g_features = [rows_of(g_stacked, m) for m in range(9)]
    g_features[0] = g_features[0] + jnp.concatenate(
        [g_refined + ro1_cols, jnp.zeros((channels, wide - atoms), F32)], axis=1
    )

    g_zero = split(g_features[0])
    g_squares = mm(sqm, g_zero, TN) * 2.0
    g_moments = [mm(mix[0], g_zero, TN)]
    for l in (1, 2):
        mixed = mm(mix[l], split(jnp.concatenate([g_features[m] for m in MEMBERS[l]], axis=1)), TN)
        g_moments += [mixed[:, i * wide : (i + 1) * wide] for i in range(len(MEMBERS[l]))]
    g_moments = [g + g_squares * moments[m] for m, g in enumerate(g_moments)]
    g_edge_one = []
    g_shapes = []
    for l in range(3):
        total = None
        for m in MEMBERS[l]:
            tiled = tile(g_moments[m])
            term = tiled if m == 0 else tiled * shapes[m]
            total = term if total is None else total + term
            if m > 0:
                g_shapes.append(jnp.sum(tiled * carried[l], axis=0, keepdims=True))
        g_edge_one.append(total * carrier)
    g_basis = radial_back(jnp.concatenate(g_edge_one, axis=0), wi1, wm1, wo1, one_g1, one_g2)

    g_basis = g_basis + spread(g_basis_two)
    g = [None] + [g_shapes[m] + spread(g_shapes_two[m]) for m in range(8)]
    g_radius = jnp.sum(g_basis * d_basis, axis=0, keepdims=True) + spread(g_radius_pair)
    gux = r3 * g[1] + r15 * (g[4] * uy + g[7] * uz + g[8] * ux) - r5 * ux * g[6]
    guy = r3 * g[2] + r15 * (g[4] * ux + g[5] * uz - g[8] * uy) - r5 * uy * g[6]
    guz = r3 * g[3] + r15 * (g[5] * uy + g[7] * ux) + 2.0 * r5 * uz * g[6]
    radial_part = g_radius - inverse * (gux * ux + guy * uy + guz * uz)
    gd = [inverse * gu + u * radial_part for gu, u in ((gux, ux), (guy, uy), (guz, uz))]
    gd = jnp.concatenate(gd + [jnp.zeros((5, gd[0].shape[1]), F32)], axis=0)
    gr = slot(gd, 0)
    for k in range(1, slots):
        gr = gr + slot(gd, k)
    to_senders = jnp.concatenate([jnp.where(domain_s == float(d), gd, 0.0) for d in range(9)], axis=0)
    to_receivers = jnp.concatenate([jnp.where(domain_r == float(d), gr, 0.0) for d in range(9)], axis=0)
    grads[...] = (
        pick(split_three(to_senders), hot_s, NT) - pick(split_three(to_receivers), hot_r, NT)
    ).reshape(9, 8, atoms)

    copies = []
    for d in others:
        copy = pltpu.make_async_remote_copy(
            src_ref=grads.at[d],
            dst_ref=back.at[8 - d],
            send_sem=send_b.at[d],
            recv_sem=recv_b.at[8 - d],
            device_id=neighbour(d),
            device_id_type=pl.DeviceIdType.MESH,
        )
        copy.start()
        copies.append(copy)
    for copy in copies:
        copy.wait()
    total = grads[4]
    for d in others:
        total = total + back[d]
    force_ref[0, 0] = -total[0:3]


def local(positions, species, senders, counts, owners, send_list, embedding,
          radial_in_one, radial_mid_one, radial_out_one, mixing, square_mix, readout_one,
          radial_in_two, radial_mid_two, radial_out_two, mix_two, read_hidden, read_out):
    atoms = positions.shape[3]
    layers = atoms // (SIDE * SIDE)
    vmem = pl.BlockSpec(memory_space=pltpu.VMEM)
    return pl.pallas_call(
        functools.partial(kernel, layers),
        out_shape=(
            jax.ShapeDtypeStruct(positions.shape, F32),
            jax.ShapeDtypeStruct(counts.shape, F32),
        ),
        in_specs=[vmem] * 19,
        out_specs=(vmem, vmem),
        scratch_shapes=[
            pltpu.VMEM((9, ROWS, atoms), F32),
            pltpu.VMEM((9, 8, atoms), F32),
            pltpu.VMEM((9, 8, atoms), F32),
            pltpu.SemaphoreType.DMA((9,)),
            pltpu.SemaphoreType.DMA((9,)),
            pltpu.SemaphoreType.DMA((9,)),
            pltpu.SemaphoreType.DMA((9,)),
        ],
        compiler_params=pltpu.CompilerParams(
            collective_id=0, has_side_effects=True, vmem_limit_bytes=48 * 1024 * 1024
        ),
    )(
        positions, species, senders, counts, owners, send_list, embedding,
        radial_in_one, radial_mid_one, radial_out_one, mixing, square_mix, readout_one[None],
        radial_in_two, radial_mid_two, radial_out_two, mix_two, read_hidden, read_out[None],
    )


def solution(mesh):
    per_domain = (
        P("gx", "gy", None, None),
        P("gx", "gy", None),
        P("gx", "gy", None, None),
        P("gx", "gy", None),
        P("gx", "gy", None, None),
        P("gx", "gy", None),
    )
    return jax.shard_map(
        local,
        mesh=mesh,
        in_specs=per_domain + (P(),) * 13,
        out_specs=(P("gx", "gy", None, None), P("gx", "gy", None)),
        check_vma=False,
    )
```

```python
import functools
import math

import jax
import jax.numpy as jnp
from jax import lax
from jax.experimental import pallas as pl
from jax.experimental.pallas import tpu as pltpu
from jax.sharding import PartitionSpec as P

SIDE = 8
SPACING = 1.75
CUTOFF = 5.0
SOFTEN = 0.25
PAIR = 2.0
ROWS = 16
DEGREE = (0, 1, 1, 1, 2, 2, 2, 2, 2)
MEMBERS = ((0,), (1, 2, 3), (4, 5, 6, 7, 8))
F32 = jnp.float32
BF16 = jnp.bfloat16
NN = (((1,), (0,)), ((), ()))
NT = (((1,), (1,)), ((), ()))


def dot(a, b, dims=NN):
    return lax.dot_general(a, b, dims, preferred_element_type=F32)


def split(x):
    high = x.astype(BF16)
    return high, (x - high.astype(F32)).astype(BF16)


def split_three(x):
    high = x.astype(BF16)
    rest = x - high.astype(F32)
    return (high,) + split(rest)


def stack_left(x):
    high, low = split(x)
    high, low = high.astype(F32), low.astype(F32)
    return jnp.concatenate([high, low, high], axis=0).T.astype(BF16)


def mm(left, b):
    high = b.astype(BF16).astype(F32)
    low = b - high
    if b.shape[0] % 16:
        right = jnp.concatenate([high, high, low], axis=0).astype(BF16)
    else:
        high, low = high.astype(BF16), low.astype(BF16)
        right = jnp.concatenate([high, high, low], axis=0)
    return dot(left, right)


def pick(parts, one_hot):
    return dot(jnp.concatenate(parts, axis=1), jnp.concatenate([one_hot] * len(parts), axis=0))


def put(parts, one_hot):
    return dot(jnp.concatenate(parts, axis=1), jnp.concatenate([one_hot] * len(parts), axis=1), NT)


def sin_cos_pi(t):
    turn = jnp.floor(t + 0.5)
    r = (t - turn) * math.pi
    sign = 1.0 - 2.0 * (turn - 2.0 * jnp.floor(turn * 0.5))
    z = r * r
    sine = jnp.full_like(z, 1.0 / math.factorial(13))
    cosine = jnp.full_like(z, -1.0 / math.factorial(14))
    for n in range(5, -1, -1):
        sine = sine * z + (-1.0) ** n / math.factorial(2 * n + 1)
    for n in range(6, -1, -1):
        cosine = cosine * z + (-1.0) ** n / math.factorial(2 * n)
    return sign * r * sine, sign * cosine


def floor_div(x, by):
    return jnp.floor((x + 0.5) * (1.0 / by))


def one_hot_rows(index, rows):
    ids = lax.broadcasted_iota(jnp.int32, (rows, index.shape[1]), 0).astype(F32)
    return jnp.where(ids == index, 1.0, 0.0).astype(BF16)


def by_domain(stacked, domain, rows):
    out = jnp.where(domain == 0.0, stacked[:rows], 0.0)
    for d in range(1, 9):
        out = out + jnp.where(domain == float(d), stacked[d * rows : (d + 1) * rows], 0.0)
    return out


def silu_pair(h):
    gate = 0.5 + 0.5 * jnp.tanh(0.5 * h)
    return h * gate, gate * (1.0 + h * (1.0 - gate))


def radial(basis, w_in, w_mid, w_out):
    s1, g1 = silu_pair(mm(w_in, basis))
    s2, g2 = silu_pair(mm(w_mid, s1))
    return mm(w_out, s2), g1, g2


def radial_back(g_out, w_in, w_mid, w_out, g1, g2):
    gh2 = mm(w_out, g_out) * g2
    gh1 = mm(w_mid, gh2) * g1
    return mm(w_in, gh1)


def kernel(
    layers,
    *refs,
):
    inputs, (force_ref, energy_ref), held = refs[:19], refs[19:21], refs[21:40]
    table, grads, back, load, send_a, recv_a, send_b, recv_b = refs[40:]
    (
        pos_ref, spec_ref, send_ref, cnt_ref, list_ref, own_ref, emb_ref,
        wi1_ref, wm1_ref, wo1_ref, mix_ref, sqm_ref, ro1_ref,
        wi2_ref, wm2_ref, wo2_ref, mx2_ref, rh_ref, ro2_ref,
    ) = held
    atoms = pos_ref.shape[3]
    bound = list_ref.shape[2]
    slots = send_ref.shape[1]
    species, channels = emb_ref.shape
    nbasis = wi1_ref.shape[0]
    column = SIDE * layers
    wide = 2 * atoms
    ring = (SIDE + 2) * layers
    used = (SIDE + 2) * ring
    me_x, me_y = lax.axis_index("gx"), lax.axis_index("gy")
    nx, ny = lax.axis_size("gx"), lax.axis_size("gy")

    def neighbour(d):
        return (lax.rem(me_x + (d // 3 - 1) + nx, nx), lax.rem(me_y + (d % 3 - 1) + ny, ny))

    others = [d for d in range(9) if d != 4]
    barrier = pltpu.get_barrier_semaphore()
    for d in others:
        pl.semaphore_signal(barrier, inc=1, device_id=neighbour(d), device_id_type=pl.DeviceIdType.MESH)

    loads = [pltpu.make_async_copy(inputs[i], held[i], load.at[i]) for i in range(19)]
    for copy in loads:
        copy.start()
    table[4] = jnp.zeros((ROWS, atoms), F32)
    for copy in loads[:5]:
        copy.wait()
    for k in range(3):
        table[4, k : k + 1, :] = pos_ref[0, k]
    table[4, 3:4, :] = spec_ref[0].astype(F32)
    for k in range(slots):
        table[4, 4 + k : 5 + k, :] = send_ref[0, k].astype(F32)
    table[4, 7:8, :] = cnt_ref[0].astype(F32)
    table[4, 8:9, 0:bound] = list_ref[0].astype(F32)
    pl.semaphore_wait(barrier, 8)
    copies = []
    for d in others:
        copy = pltpu.make_async_remote_copy(
            src_ref=table.at[4],
            dst_ref=table.at[8 - d],
            send_sem=send_a.at[d],
            recv_sem=recv_a.at[8 - d],
            device_id=neighbour(d),
            device_id_type=pl.DeviceIdType.MESH,
        )
        copy.start()
        copies.append(copy)

    lane = lax.broadcasted_iota(jnp.int32, (1, wide), 1).astype(F32)
    ring_at = lane - atoms
    low_x = ring_at < ring
    long_side = ring_at < 2 * ring
    along = jnp.where(low_x, ring_at, ring_at - ring)
    in_y = ring_at - 2 * ring
    low_y = in_y < column
    across = jnp.where(low_y, in_y, in_y - column)
    half_long = floor_div(along, layers)
    half_short = floor_div(across, layers)
    site_x = jnp.where(long_side, jnp.where(low_x, -1.0, float(SIDE)), half_short)
    site_y = jnp.where(long_side, half_long - 1.0, jnp.where(low_y, -1.0, float(SIDE)))
    site_z = jnp.where(long_side, along - half_long * layers, across - half_short * layers)
    inside = (lane < atoms) | (lane >= used)
    off_x = jnp.where(inside, 0.0, floor_div(site_x, SIDE))
    off_y = jnp.where(inside, 0.0, floor_div(site_y, SIDE))
    ring_atom = (site_x - off_x * SIDE) * column + (site_y - off_y * SIDE) * layers + site_z
    atom_r = jnp.where(lane < atoms, lane, jnp.where(lane >= used, 0.0, ring_atom))
    domain_r = 3.0 * (off_x + 1.0) + (off_y + 1.0)
    hot_r = one_hot_rows(atom_r, atoms)

    for copy in loads[5:]:
        copy.wait()
    wi1, wi1_back = stack_left(wi1_ref[...]), stack_left(wi1_ref[...].T)
    wi2, wi2_back = stack_left(wi2_ref[...]), stack_left(wi2_ref[...].T)
    wm1, wm1_back = stack_left(wm1_ref[...].T), stack_left(wm1_ref[...])
    wm2, wm2_back = stack_left(wm2_ref[...].T), stack_left(wm2_ref[...])
    wo1, wo1_back = stack_left(wo1_ref[...]), stack_left(wo1_ref[...].T)
    wo2, wo2_back = stack_left(wo2_ref[...]), stack_left(wo2_ref[...].T)
    mix = [stack_left(mix_ref[l].T) for l in range(3)]
    mix_back = [stack_left(mix_ref[l]) for l in range(3)]
    sqm, sqm_back = stack_left(sqm_ref[...].T), stack_left(sqm_ref[...])
    mx2, mx2_back = stack_left(mx2_ref[...].T), stack_left(mx2_ref[...])
    rh, rh_back = stack_left(rh_ref[...].T), stack_left(rh_ref[...])
    emb = split_three(emb_ref[...].T)
    ro1_cols = jnp.broadcast_to(ro1_ref[...], (atoms, channels)).T
    ro2_cols = jnp.broadcast_to(ro2_ref[...], (atoms, ro2_ref.shape[1])).T

    for copy in copies:
        copy.wait()

    def tile(x):
        return jnp.concatenate([x] * slots, axis=1)

    def slot(x, k):
        return x[:, k * wide : (k + 1) * wide]

    def own(x):
        return jnp.concatenate([x[:, k * wide : k * wide + atoms] for k in range(slots)], axis=1)

    def own_slot(x, k):
        return x[:, k * atoms : (k + 1) * atoms]

    def spread(x):
        zero = jnp.zeros((x.shape[0], atoms), F32)
        return jnp.concatenate([p for k in range(slots) for p in (own_slot(x, k), zero)], axis=1)

    everything = table[...].reshape(9 * ROWS, atoms)
    parts = split_three(everything)
    rec = by_domain(pick(parts, hot_r), domain_r, ROWS)
    sender = jnp.concatenate([rec[4 + k : 5 + k] for k in range(slots)], axis=1)
    live = jnp.concatenate(
        [jnp.where((rec[7:8] > float(k)) & (lane < used), 1.0, 0.0) for k in range(slots)], axis=1
    )
    is_local = sender < atoms
    ghost = sender - atoms
    block = floor_div(ghost, bound)
    place = ghost - block * bound
    block = jnp.where(block >= 4.0, block + 1.0, block)
    block = jnp.where(is_local, 4.0, block)
    block_x = floor_div(block, 3)
    block_y = block - 3.0 * block_x - 1.0
    block_x = block_x - 1.0
    to_x = tile(off_x) + block_x
    to_y = tile(off_y) + block_y
    domain_s = 3.0 * (to_x + 1.0) + (to_y + 1.0)
    lists = dot(parts[0], one_hot_rows(place, atoms))
    listed = jnp.zeros_like(sender)
    for d in range(9):
        listed = listed + jnp.where(domain_s == float(d), lists[d * ROWS + 8 : d * ROWS + 9], 0.0)
    atom_s = jnp.where(is_local, sender, listed)
    hot_s = one_hot_rows(atom_s, atoms)
    upper = jnp.concatenate([table[d, 0:8, :] for d in range(9)], axis=0)
    snd = by_domain(pick(split_three(upper), hot_s), domain_s, 8)

    side_length = SPACING * SIDE
    dx = (snd[0:1] + block_x * side_length) - tile(rec[0:1])
    dy = (snd[1:2] + block_y * side_length) - tile(rec[1:2])
    dz = snd[2:3] - tile(rec[2:3])
    radius = jnp.sqrt(dx * dx + dy * dy + dz * dz + SOFTEN)
    inverse = 1.0 / radius
    ux, uy, uz = dx * inverse, dy * inverse, dz * inverse
    x = jnp.minimum(radius / CUTOFF, 1.0)
    x2 = x * x
    x5 = x2 * x2 * x
    x6 = x5 * x
    envelope = 1.0 + x6 * (-28.0 + x * (48.0 - 21.0 * x))
    slope = jnp.where(radius < CUTOFF, 1.0 / CUTOFF, 0.0)
    d_envelope = x5 * (-168.0 + x * (336.0 - 168.0 * x)) * slope
    orders = (lax.broadcasted_iota(jnp.int32, (nbasis, 1), 0) + 1).astype(F32)
    scale = math.sqrt(2.0 / CUTOFF)
    sines, cosines = sin_cos_pi(orders * x)
    sines = sines * scale
    cosines = cosines * (orders * (scale * math.pi))
    basis = sines * (inverse * envelope)
    d_basis = cosines * (slope * inverse * envelope) + sines * (
        inverse * d_envelope - inverse * inverse * envelope
    )
    r3, r5, r15 = math.sqrt(3.0), math.sqrt(5.0), math.sqrt(15.0)
    shapes = [
        None,
        r3 * ux,
        r3 * uy,
        r3 * uz,
        r15 * ux * uy,
        r15 * uy * uz,
        0.5 * r5 * (2.0 * uz * uz - ux * ux - uy * uy),
        r15 * ux * uz,
        0.5 * r15 * (ux * ux - uy * uy),
    ]

    def rows_of(w, l):
        return w[l * channels : (l + 1) * channels]

    species_row = lax.broadcasted_iota(jnp.int32, (species, 1), 0).astype(F32)
    hot_es = jnp.where(species_row == snd[3:4], 1.0, 0.0).astype(BF16)
    hot_er = jnp.where(species_row == rec[3:4], 1.0, 0.0).astype(BF16)
    carrier = pick(emb, hot_es) * (live * (1.0 / slots))
    embedded = pick(emb, hot_er)
    edge_one, one_g1, one_g2 = radial(basis, wi1, wm1, wo1)
    carried = [rows_of(edge_one, l) * carrier for l in range(3)]
    moments = []
    for m in range(9):
        term = carried[DEGREE[m]] if m == 0 else carried[DEGREE[m]] * shapes[m]
        total = slot(term, 0)
        for k in range(1, slots):
            total = total + slot(term, k)
        moments.append(total)
    squares = moments[0] * moments[0]
    for m in range(1, 9):
        squares = squares + moments[m] * moments[m]
    features = [mm(mix[0], moments[0]) + mm(sqm, squares) + embedded]
    for l in (1, 2):
        mixed = mm(mix[l], jnp.concatenate([moments[m] for m in MEMBERS[l]], axis=1))
        features += [mixed[:, i * wide : (i + 1) * wide] for i in range(len(MEMBERS[l]))]

    live_two = own(live) * (1.0 / slots)
    edge_two, two_g1, two_g2 = radial(own(basis), wi2, wm2, wo2)
    shapes_two = [None] + [own(s) for s in shapes[1:]]
    at_two, to_x2, to_y2 = own(atom_s), own(to_x), own(to_y)
    ax = floor_div(at_two, column)
    rest = at_two - ax * column
    ay = floor_div(rest, layers)
    az = rest - ay * layers
    sx = ax + to_x2 * SIDE
    sy = ay + to_y2 * SIDE
    outside = jnp.where(
        to_x2 != 0.0,
        jnp.where(to_x2 < 0.0, 0.0, float(ring)) + (sy + 1.0) * layers + az,
        2.0 * ring + jnp.where(to_y2 < 0.0, 0.0, float(column)) + sx * layers + az,
    )
    at_ring = jnp.where((to_x2 == 0.0) & (to_y2 == 0.0), at_two, atoms + outside)
    hot_two = one_hot_rows(at_ring, wide)
    stacked = jnp.concatenate(features, axis=0)
    sent = pick(split(stacked), hot_two)
    projected = []
    for l in range(3):
        total = None
        for m in MEMBERS[l]:
            term = rows_of(sent, m) if m == 0 else rows_of(sent, m) * shapes_two[m]
            total = term if total is None else total + term
        projected.append(total)
    scalar = sum(rows_of(edge_two, l) * projected[l] for l in range(3)) * live_two
    gathered = own_slot(scalar, 0)
    for k in range(1, slots):
        gathered = gathered + own_slot(scalar, k)
    refined = mm(mx2, gathered) + features[0][:, :atoms]
    hidden, hidden_slope = silu_pair(mm(rh, refined))
    energy_two = jnp.sum(ro2_cols * hidden, axis=0, keepdims=True)
    energy_one = jnp.sum(ro1_cols * features[0][:, :atoms], axis=0, keepdims=True)
    owners = jnp.concatenate([own_ref[0, k].astype(F32) for k in range(slots)], axis=1)
    decay = PAIR * jnp.exp(-own(radius)) * owners * own(live)
    pair = decay * own(envelope)
    energy = energy_one + energy_two
    for k in range(slots):
        energy = energy + own_slot(pair, k)
    energy_ref[0] = energy
    g_radius_pair = decay * (own(d_envelope) - own(envelope))

    g_refined = mm(rh_back, ro2_cols * hidden_slope)
    g_gathered = mm(mx2_back, g_refined)
    t = jnp.concatenate([g_gathered] * slots, axis=1) * live_two
    g_edge_two = jnp.concatenate([t * projected[l] for l in range(3)], axis=0)
    g_proj = [t * rows_of(edge_two, l) for l in range(3)]
    g_sent = jnp.concatenate(
        [g_proj[0]] + [g_proj[DEGREE[m]] * shapes_two[m] for m in range(1, 9)], axis=0
    )
    g_shapes_two = [
        jnp.sum(g_proj[DEGREE[m]] * rows_of(sent, m), axis=0, keepdims=True) for m in range(1, 9)
    ]
    g_basis_two = radial_back(g_edge_two, wi2_back, wm2_back, wo2_back, two_g1, two_g2)
    g_stacked = put(split(g_sent), hot_two)
    g_features = [rows_of(g_stacked, m) for m in range(9)]
    g_features[0] = g_features[0] + jnp.concatenate(
        [g_refined + ro1_cols, jnp.zeros((channels, wide - atoms), F32)], axis=1
    )

    g_squares = mm(sqm_back, g_features[0]) * 2.0
    g_moments = [mm(mix_back[0], g_features[0])]
    for l in (1, 2):
        mixed = mm(mix_back[l], jnp.concatenate([g_features[m] for m in MEMBERS[l]], axis=1))
        g_moments += [mixed[:, i * wide : (i + 1) * wide] for i in range(len(MEMBERS[l]))]
    g_moments = [g + g_squares * moments[m] for m, g in enumerate(g_moments)]
    g_edge_one = []
    g_shapes = []
    for l in range(3):
        total = None
        for m in MEMBERS[l]:
            tiled = tile(g_moments[m])
            term = tiled if m == 0 else tiled * shapes[m]
            total = term if total is None else total + term
            if m > 0:
                g_shapes.append(jnp.sum(tiled * carried[l], axis=0, keepdims=True))
        g_edge_one.append(total * carrier)
    g_basis = radial_back(
        jnp.concatenate(g_edge_one, axis=0), wi1_back, wm1_back, wo1_back, one_g1, one_g2
    )

    g_basis = g_basis + spread(g_basis_two)
    g = [None] + [g_shapes[m] + spread(g_shapes_two[m]) for m in range(8)]
    g_radius = jnp.sum(g_basis * d_basis, axis=0, keepdims=True) + spread(g_radius_pair)
    gux = r3 * g[1] + r15 * (g[4] * uy + g[7] * uz + g[8] * ux) - r5 * ux * g[6]
    guy = r3 * g[2] + r15 * (g[4] * ux + g[5] * uz - g[8] * uy) - r5 * uy * g[6]
    guz = r3 * g[3] + r15 * (g[5] * uy + g[7] * ux) + 2.0 * r5 * uz * g[6]
    radial_part = g_radius - inverse * (gux * ux + guy * uy + guz * uz)
    gd = [inverse * gu + u * radial_part for gu, u in ((gux, ux), (guy, uy), (guz, uz))]
    gd = jnp.concatenate(gd + [jnp.zeros((5, gd[0].shape[1]), F32)], axis=0)
    gr = slot(gd, 0)
    for k in range(1, slots):
        gr = gr + slot(gd, k)
    to_senders = jnp.concatenate([jnp.where(domain_s == float(d), gd, 0.0) for d in range(9)], axis=0)
    to_receivers = jnp.concatenate([jnp.where(domain_r == float(d), gr, 0.0) for d in range(9)], axis=0)
    grads[...] = (
        put(split(to_senders), hot_s) - put(split(to_receivers), hot_r)
    ).reshape(9, 8, atoms)

    copies = []
    for d in others:
        copy = pltpu.make_async_remote_copy(
            src_ref=grads.at[d],
            dst_ref=back.at[8 - d],
            send_sem=send_b.at[d],
            recv_sem=recv_b.at[8 - d],
            device_id=neighbour(d),
            device_id_type=pl.DeviceIdType.MESH,
        )
        copy.start()
        copies.append(copy)
    for copy in copies:
        copy.wait()
    total = grads[4]
    for d in others:
        total = total + back[d]
    for k in range(3):
        force_ref[0, k] = -total[k : k + 1]


def local(positions, species, senders, counts, owners, send_list, embedding,
          radial_in_one, radial_mid_one, radial_out_one, mixing, square_mix, readout_one,
          radial_in_two, radial_mid_two, radial_out_two, mix_two, read_hidden, read_out):
    atoms = positions.shape[3]
    layers = atoms // (SIDE * SIDE)
    operands = (
        positions.transpose(0, 2, 1, 3), species, senders.transpose(0, 2, 1, 3), counts, send_list,
        owners.transpose(0, 2, 1, 3), embedding.T,
        radial_in_one.T, radial_mid_one, radial_out_one.T, mixing, square_mix, readout_one[None],
        radial_in_two.T, radial_mid_two, radial_out_two.T, mix_two, read_hidden, read_out[None],
    )
    vmem = pl.BlockSpec(memory_space=pltpu.VMEM)
    forces, energies = pl.pallas_call(
        functools.partial(kernel, layers),
        out_shape=(
            jax.ShapeDtypeStruct(operands[0].shape, F32),
            jax.ShapeDtypeStruct(counts.shape, F32),
        ),
        in_specs=[pl.BlockSpec(memory_space=pltpu.HBM)] * len(operands),
        out_specs=(vmem, vmem),
        scratch_shapes=[pltpu.VMEM(x.shape, x.dtype) for x in operands]
        + [
            pltpu.VMEM((9, ROWS, atoms), F32),
            pltpu.VMEM((9, 8, atoms), F32),
            pltpu.VMEM((9, 8, atoms), F32),
            pltpu.SemaphoreType.DMA((len(operands),)),
            pltpu.SemaphoreType.DMA((9,)),
            pltpu.SemaphoreType.DMA((9,)),
            pltpu.SemaphoreType.DMA((9,)),
            pltpu.SemaphoreType.DMA((9,)),
        ],
        compiler_params=pltpu.CompilerParams(
            collective_id=0, has_side_effects=True, vmem_limit_bytes=64 * 1024 * 1024
        ),
    )(*operands)
    return forces.transpose(0, 2, 1, 3), energies


def solution(mesh):
    per_domain = (
        P("gx", "gy", None, None),
        P("gx", "gy", None),
        P("gx", "gy", None, None),
        P("gx", "gy", None),
        P("gx", "gy", None, None),
        P("gx", "gy", None),
    )
    return jax.shard_map(
        local,
        mesh=mesh,
        in_specs=per_domain + (P(),) * 13,
        out_specs=(P("gx", "gy", None, None), P("gx", "gy", None)),
        check_vma=False,
    )
```

```python
import functools
import math

import jax
import jax.numpy as jnp
from jax import lax
from jax.experimental import pallas as pl
from jax.experimental.pallas import tpu as pltpu
from jax.sharding import PartitionSpec as P

SIDE = 8
SPACING = 1.75
CUTOFF = 5.0
SOFTEN = 0.25
PAIR = 2.0
ROWS = 16
DEGREE = (0, 1, 1, 1, 2, 2, 2, 2, 2)
MEMBERS = ((0,), (1, 2, 3), (4, 5, 6, 7, 8))
F32 = jnp.float32
BF16 = jnp.bfloat16
NN = (((1,), (0,)), ((), ()))
NT = (((1,), (1,)), ((), ()))


def dot(a, b, dims=NN):
    return lax.dot_general(a, b, dims, preferred_element_type=F32)


def split(x):
    high = x.astype(BF16)
    return high, (x - high.astype(F32)).astype(BF16)


def split_three(x):
    high = x.astype(BF16)
    rest = x - high.astype(F32)
    return (high,) + split(rest)


def stack_left(x):
    high, low = split(x)
    high, low = high.astype(F32), low.astype(F32)
    return jnp.concatenate([high, low, high], axis=0).T.astype(BF16)


def mm(left, b):
    high = b.astype(BF16).astype(F32)
    low = b - high
    if b.shape[0] % 16:
        right = jnp.concatenate([high, high, low], axis=0).astype(BF16)
    else:
        high, low = high.astype(BF16), low.astype(BF16)
        right = jnp.concatenate([high, high, low], axis=0)
    return dot(left, right)


def pick(parts, one_hot):
    return dot(jnp.concatenate(parts, axis=1), jnp.concatenate([one_hot] * len(parts), axis=0))


def put(parts, one_hot):
    return dot(jnp.concatenate(parts, axis=1), jnp.concatenate([one_hot] * len(parts), axis=1), NT)


def sin_cos_pi(t):
    turn = jnp.floor(t + 0.5)
    r = (t - turn) * math.pi
    sign = 1.0 - 2.0 * (turn - 2.0 * jnp.floor(turn * 0.5))
    z = r * r
    sine = jnp.full_like(z, 1.0 / math.factorial(13))
    cosine = jnp.full_like(z, -1.0 / math.factorial(14))
    for n in range(5, -1, -1):
        sine = sine * z + (-1.0) ** n / math.factorial(2 * n + 1)
    for n in range(6, -1, -1):
        cosine = cosine * z + (-1.0) ** n / math.factorial(2 * n)
    return sign * r * sine, sign * cosine


def floor_div(x, by):
    return jnp.floor((x + 0.5) * (1.0 / by))


def one_hot_rows(index, rows):
    ids = lax.broadcasted_iota(jnp.int32, (rows, index.shape[1]), 0).astype(F32)
    return jnp.where(ids == index, 1.0, 0.0).astype(BF16)


def by_domain(stacked, domain, rows):
    out = jnp.where(domain == 0.0, stacked[:rows], 0.0)
    for d in range(1, 9):
        out = out + jnp.where(domain == float(d), stacked[d * rows : (d + 1) * rows], 0.0)
    return out


def silu_pair(h):
    gate = 0.5 + 0.5 * jnp.tanh(0.5 * h)
    return h * gate, gate * (1.0 + h * (1.0 - gate))


def radial(basis, w_in, w_mid, w_out):
    s1, g1 = silu_pair(mm(w_in, basis))
    s2, g2 = silu_pair(mm(w_mid, s1))
    return mm(w_out, s2), g1, g2


def radial_back(g_out, w_in, w_mid, w_out, g1, g2):
    gh2 = mm(w_out, g_out) * g2
    gh1 = mm(w_mid, gh2) * g1
    return mm(w_in, gh1)


def kernel(
    layers,
    *refs,
):
    inputs, out_ref, held = refs[:19], refs[19], refs[20:39]
    table, grads, back, load, send_a, recv_a, send_b, recv_b = refs[39:47]
    basis_s, shape_s, edge_s, gate_s, carrier_s, carried_s, moment_s, g_moment_s, g_basis_s, g_shape_s = (
        refs[47:]
    )
    (
        pos_ref, spec_ref, send_ref, cnt_ref, list_ref, own_ref, emb_ref,
        wi1_ref, wm1_ref, wo1_ref, mix_ref, sqm_ref, ro1_ref,
        wi2_ref, wm2_ref, wo2_ref, mx2_ref, rh_ref, ro2_ref,
    ) = held
    atoms = pos_ref.shape[3]
    bound = list_ref.shape[2]
    slots = send_ref.shape[1]
    species, channels = emb_ref.shape
    nbasis = wi1_ref.shape[0]
    column = SIDE * layers
    wide = 2 * atoms
    ring = (SIDE + 2) * layers
    used = (SIDE + 2) * ring
    me_x, me_y = lax.axis_index("gx"), lax.axis_index("gy")
    nx, ny = lax.axis_size("gx"), lax.axis_size("gy")

    def neighbour(d):
        return (lax.rem(me_x + (d // 3 - 1) + nx, nx), lax.rem(me_y + (d % 3 - 1) + ny, ny))

    others = [d for d in range(9) if d != 4]
    barrier = pltpu.get_barrier_semaphore()
    for d in others:
        pl.semaphore_signal(barrier, inc=1, device_id=neighbour(d), device_id_type=pl.DeviceIdType.MESH)

    loads = [pltpu.make_async_copy(inputs[i], held[i], load.at[i]) for i in range(19)]
    for copy in loads:
        copy.start()
    table[4] = jnp.zeros((ROWS, atoms), F32)
    for copy in loads[:5]:
        copy.wait()
    for k in range(3):
        table[4, k : k + 1, :] = pos_ref[0, k]
    table[4, 3:4, :] = spec_ref[0].astype(F32)
    for k in range(slots):
        table[4, 4 + k : 5 + k, :] = send_ref[0, k].astype(F32)
    table[4, 7:8, :] = cnt_ref[0].astype(F32)
    table[4, 8:9, 0:bound] = list_ref[0].astype(F32)
    pl.semaphore_wait(barrier, 8)
    copies = []
    for d in others:
        copy = pltpu.make_async_remote_copy(
            src_ref=table.at[4],
            dst_ref=table.at[8 - d],
            send_sem=send_a.at[d],
            recv_sem=recv_a.at[8 - d],
            device_id=neighbour(d),
            device_id_type=pl.DeviceIdType.MESH,
        )
        copy.start()
        copies.append(copy)

    lane = lax.broadcasted_iota(jnp.int32, (1, wide), 1).astype(F32)
    ring_at = lane - atoms
    low_x = ring_at < ring
    long_side = ring_at < 2 * ring
    along = jnp.where(low_x, ring_at, ring_at - ring)
    in_y = ring_at - 2 * ring
    low_y = in_y < column
    across = jnp.where(low_y, in_y, in_y - column)
    half_long = floor_div(along, layers)
    half_short = floor_div(across, layers)
    site_x = jnp.where(long_side, jnp.where(low_x, -1.0, float(SIDE)), half_short)
    site_y = jnp.where(long_side, half_long - 1.0, jnp.where(low_y, -1.0, float(SIDE)))
    site_z = jnp.where(long_side, along - half_long * layers, across - half_short * layers)
    inside = (lane < atoms) | (lane >= used)
    off_x = jnp.where(inside, 0.0, floor_div(site_x, SIDE))
    off_y = jnp.where(inside, 0.0, floor_div(site_y, SIDE))
    ring_atom = (site_x - off_x * SIDE) * column + (site_y - off_y * SIDE) * layers + site_z
    atom_r = jnp.where(lane < atoms, lane, jnp.where(lane >= used, 0.0, ring_atom))
    domain_r = 3.0 * (off_x + 1.0) + (off_y + 1.0)
    hot_r = one_hot_rows(atom_r, atoms)

    for copy in loads[5:]:
        copy.wait()
    wi1, wi1_back = stack_left(wi1_ref[...]), stack_left(wi1_ref[...].T)
    wi2, wi2_back = stack_left(wi2_ref[...]), stack_left(wi2_ref[...].T)
    wm1, wm1_back = stack_left(wm1_ref[...].T), stack_left(wm1_ref[...])
    wm2, wm2_back = stack_left(wm2_ref[...].T), stack_left(wm2_ref[...])
    wo1, wo1_back = stack_left(wo1_ref[...]), stack_left(wo1_ref[...].T)
    wo2, wo2_back = stack_left(wo2_ref[...]), stack_left(wo2_ref[...].T)
    mix = [stack_left(mix_ref[l].T) for l in range(3)]
    mix_back = [stack_left(mix_ref[l]) for l in range(3)]
    sqm, sqm_back = stack_left(sqm_ref[...].T), stack_left(sqm_ref[...])
    mx2, mx2_back = stack_left(mx2_ref[...].T), stack_left(mx2_ref[...])
    rh, rh_back = stack_left(rh_ref[...].T), stack_left(rh_ref[...])
    emb = split_three(emb_ref[...].T)
    ro1_cols = jnp.broadcast_to(ro1_ref[...], (atoms, channels)).T
    ro2_cols = jnp.broadcast_to(ro2_ref[...], (atoms, ro2_ref.shape[1])).T

    for copy in copies:
        copy.wait()

    def tile(x):
        return jnp.concatenate([x] * slots, axis=1)

    def slot(x, k):
        return x[:, k * wide : (k + 1) * wide]

    def own(x):
        return jnp.concatenate([x[:, k * wide : k * wide + atoms] for k in range(slots)], axis=1)

    def own_slot(x, k):
        return x[:, k * atoms : (k + 1) * atoms]

    def spread(x):
        zero = jnp.zeros((x.shape[0], atoms), F32)
        return jnp.concatenate([p for k in range(slots) for p in (own_slot(x, k), zero)], axis=1)

    everything = table[...].reshape(9 * ROWS, atoms)
    parts = split_three(everything)
    rec = by_domain(pick(parts, hot_r), domain_r, ROWS)
    sender = jnp.concatenate([rec[4 + k : 5 + k] for k in range(slots)], axis=1)
    live = jnp.concatenate(
        [jnp.where((rec[7:8] > float(k)) & (lane < used), 1.0, 0.0) for k in range(slots)], axis=1
    )
    is_local = sender < atoms
    ghost = sender - atoms
    block = floor_div(ghost, bound)
    place = ghost - block * bound
    block = jnp.where(block >= 4.0, block + 1.0, block)
    block = jnp.where(is_local, 4.0, block)
    block_x = floor_div(block, 3)
    block_y = block - 3.0 * block_x - 1.0
    block_x = block_x - 1.0
    to_x = tile(off_x) + block_x
    to_y = tile(off_y) + block_y
    domain_s = 3.0 * (to_x + 1.0) + (to_y + 1.0)
    lists = dot(parts[0], one_hot_rows(place, atoms))
    listed = jnp.zeros_like(sender)
    for d in range(9):
        listed = listed + jnp.where(domain_s == float(d), lists[d * ROWS + 8 : d * ROWS + 9], 0.0)
    atom_s = jnp.where(is_local, sender, listed)
    hot_s = one_hot_rows(atom_s, atoms)
    upper = jnp.concatenate([table[d, 0:8, :] for d in range(9)], axis=0)
    snd = by_domain(pick(split_three(upper), hot_s), domain_s, 8)

    side_length = SPACING * SIDE
    dx = (snd[0:1] + block_x * side_length) - tile(rec[0:1])
    dy = (snd[1:2] + block_y * side_length) - tile(rec[1:2])
    dz = snd[2:3] - tile(rec[2:3])
    radius = jnp.sqrt(dx * dx + dy * dy + dz * dz + SOFTEN)
    inverse = 1.0 / radius
    ux, uy, uz = dx * inverse, dy * inverse, dz * inverse
    x = jnp.minimum(radius / CUTOFF, 1.0)
    x2 = x * x
    x5 = x2 * x2 * x
    x6 = x5 * x
    envelope = 1.0 + x6 * (-28.0 + x * (48.0 - 21.0 * x))
    slope = jnp.where(radius < CUTOFF, 1.0 / CUTOFF, 0.0)
    d_envelope = x5 * (-168.0 + x * (336.0 - 168.0 * x)) * slope
    orders = (lax.broadcasted_iota(jnp.int32, (nbasis, 1), 0) + 1).astype(F32)
    scale = math.sqrt(2.0 / CUTOFF)
    sines, cosines = sin_cos_pi(orders * x)
    sines = sines * scale
    cosines = cosines * (orders * (scale * math.pi))
    basis = sines * (inverse * envelope)
    d_basis = cosines * (slope * inverse * envelope) + sines * (
        inverse * d_envelope - inverse * inverse * envelope
    )
    r3, r5, r15 = math.sqrt(3.0), math.sqrt(5.0), math.sqrt(15.0)
    shapes = [
        None,
        r3 * ux,
        r3 * uy,
        r3 * uz,
        r15 * ux * uy,
        r15 * uy * uz,
        0.5 * r5 * (2.0 * uz * uz - ux * ux - uy * uy),
        r15 * ux * uz,
        0.5 * r15 * (ux * ux - uy * uy),
    ]

    def rows_of(w, l):
        return w[l * channels : (l + 1) * channels]

    shapes_all = jnp.concatenate(shapes[1:], axis=0)
    live_one = live * (1.0 / slots)
    for k in range(slots):
        basis_s[k] = slot(basis, k)
        shape_s[k] = slot(shapes_all, k)
        edge_s[k, 0:1, :] = slot(snd[3:4], k)
        edge_s[k, 1:2, :] = slot(live_one, k)
    species_row = lax.broadcasted_iota(jnp.int32, (species, 1), 0).astype(F32)
    hot_er = jnp.where(species_row == rec[3:4], 1.0, 0.0).astype(BF16)
    embedded = pick(emb, hot_er)
    moment_s[...] = jnp.zeros(moment_s.shape, F32)

    def forward(k, carry):
        hot_es = jnp.where(species_row == edge_s[k, 0:1, :], 1.0, 0.0).astype(BF16)
        carrier = pick(emb, hot_es) * edge_s[k, 1:2, :]
        carrier_s[k] = carrier
        edge, g1, g2 = radial(basis_s[k], wi1, wm1, wo1)
        gate_s[k, 0] = g1
        gate_s[k, 1] = g2
        shape = shape_s[k]
        for l in range(3):
            carried = rows_of(edge, l) * carrier
            carried_s[k, l] = carried
            for m in MEMBERS[l]:
                term = carried if m == 0 else carried * shape[m - 1 : m]
                moment_s[m] = moment_s[m] + term
        return carry

    lax.fori_loop(0, slots, forward, 0)
    moments = [moment_s[m] for m in range(9)]
    squares = moments[0] * moments[0]
    for m in range(1, 9):
        squares = squares + moments[m] * moments[m]
    features = [mm(mix[0], moments[0]) + mm(sqm, squares) + embedded]
    for l in (1, 2):
        mixed = mm(mix[l], jnp.concatenate([moments[m] for m in MEMBERS[l]], axis=1))
        features += [mixed[:, i * wide : (i + 1) * wide] for i in range(len(MEMBERS[l]))]

    live_two = own(live) * (1.0 / slots)
    edge_two, two_g1, two_g2 = radial(own(basis), wi2, wm2, wo2)
    shapes_two = [None] + [own(s) for s in shapes[1:]]
    at_two, to_x2, to_y2 = own(atom_s), own(to_x), own(to_y)
    ax = floor_div(at_two, column)
    rest = at_two - ax * column
    ay = floor_div(rest, layers)
    az = rest - ay * layers
    sx = ax + to_x2 * SIDE
    sy = ay + to_y2 * SIDE
    outside = jnp.where(
        to_x2 != 0.0,
        jnp.where(to_x2 < 0.0, 0.0, float(ring)) + (sy + 1.0) * layers + az,
        2.0 * ring + jnp.where(to_y2 < 0.0, 0.0, float(column)) + sx * layers + az,
    )
    at_ring = jnp.where((to_x2 == 0.0) & (to_y2 == 0.0), at_two, atoms + outside)
    hot_two = one_hot_rows(at_ring, wide)
    stacked = jnp.concatenate(features, axis=0)
    sent = pick(split(stacked), hot_two)
    projected = []
    for l in range(3):
        total = None
        for m in MEMBERS[l]:
            term = rows_of(sent, m) if m == 0 else rows_of(sent, m) * shapes_two[m]
            total = term if total is None else total + term
        projected.append(total)
    scalar = sum(rows_of(edge_two, l) * projected[l] for l in range(3)) * live_two
    gathered = own_slot(scalar, 0)
    for k in range(1, slots):
        gathered = gathered + own_slot(scalar, k)
    refined = mm(mx2, gathered) + features[0][:, :atoms]
    hidden, hidden_slope = silu_pair(mm(rh, refined))
    energy_two = jnp.sum(ro2_cols * hidden, axis=0, keepdims=True)
    energy_one = jnp.sum(ro1_cols * features[0][:, :atoms], axis=0, keepdims=True)
    owners = jnp.concatenate([own_ref[0, k].astype(F32) for k in range(slots)], axis=1)
    decay = PAIR * jnp.exp(-own(radius)) * owners * own(live)
    pair = decay * own(envelope)
    energy = energy_one + energy_two
    for k in range(slots):
        energy = energy + own_slot(pair, k)
    out_ref[0, 3] = energy
    g_radius_pair = decay * (own(d_envelope) - own(envelope))

    g_refined = mm(rh_back, ro2_cols * hidden_slope)
    g_gathered = mm(mx2_back, g_refined)
    t = jnp.concatenate([g_gathered] * slots, axis=1) * live_two
    g_edge_two = jnp.concatenate([t * projected[l] for l in range(3)], axis=0)
    g_proj = [t * rows_of(edge_two, l) for l in range(3)]
    g_sent = jnp.concatenate(
        [g_proj[0]] + [g_proj[DEGREE[m]] * shapes_two[m] for m in range(1, 9)], axis=0
    )
    g_shapes_two = [
        jnp.sum(g_proj[DEGREE[m]] * rows_of(sent, m), axis=0, keepdims=True) for m in range(1, 9)
    ]
    g_basis_two = radial_back(g_edge_two, wi2_back, wm2_back, wo2_back, two_g1, two_g2)
    g_stacked = put(split(g_sent), hot_two)
    g_features = [rows_of(g_stacked, m) for m in range(9)]
    g_features[0] = g_features[0] + jnp.concatenate(
        [g_refined + ro1_cols, jnp.zeros((channels, wide - atoms), F32)], axis=1
    )

    g_squares = mm(sqm_back, g_features[0]) * 2.0
    g_moments = [mm(mix_back[0], g_features[0])]
    for l in (1, 2):
        mixed = mm(mix_back[l], jnp.concatenate([g_features[m] for m in MEMBERS[l]], axis=1))
        g_moments += [mixed[:, i * wide : (i + 1) * wide] for i in range(len(MEMBERS[l]))]
    for m in range(9):
        g_moment_s[m] = g_moments[m] + g_squares * moment_s[m]

    def backward(k, carry):
        carrier = carrier_s[k]
        shape = shape_s[k]
        g_edge = []
        g_shape = []
        for l in range(3):
            carried = carried_s[k, l]
            total = None
            for m in MEMBERS[l]:
                g_m = g_moment_s[m]
                term = g_m if m == 0 else g_m * shape[m - 1 : m]
                total = term if total is None else total + term
                if m > 0:
                    g_shape.append(jnp.sum(g_m * carried, axis=0, keepdims=True))
            g_edge.append(total * carrier)
        g_shape_s[k] = jnp.concatenate(g_shape, axis=0)
        g_basis_s[k] = radial_back(
            jnp.concatenate(g_edge, axis=0), wi1_back, wm1_back, wo1_back, gate_s[k, 0], gate_s[k, 1]
        )
        return carry

    lax.fori_loop(0, slots, backward, 0)
    g_basis = jnp.concatenate([g_basis_s[k] for k in range(slots)], axis=1)
    g_shapes_all = jnp.concatenate([g_shape_s[k] for k in range(slots)], axis=1)
    g_shapes = [g_shapes_all[m : m + 1] for m in range(8)]

    g_basis = g_basis + spread(g_basis_two)
    g = [None] + [g_shapes[m] + spread(g_shapes_two[m]) for m in range(8)]
    g_radius = jnp.sum(g_basis * d_basis, axis=0, keepdims=True) + spread(g_radius_pair)
    gux = r3 * g[1] + r15 * (g[4] * uy + g[7] * uz + g[8] * ux) - r5 * ux * g[6]
    guy = r3 * g[2] + r15 * (g[4] * ux + g[5] * uz - g[8] * uy) - r5 * uy * g[6]
    guz = r3 * g[3] + r15 * (g[5] * uy + g[7] * ux) + 2.0 * r5 * uz * g[6]
    radial_part = g_radius - inverse * (gux * ux + guy * uy + guz * uz)
    gd = [inverse * gu + u * radial_part for gu, u in ((gux, ux), (guy, uy), (guz, uz))]
    gd = jnp.concatenate(gd + [jnp.zeros((5, gd[0].shape[1]), F32)], axis=0)
    gr = slot(gd, 0)
    for k in range(1, slots):
        gr = gr + slot(gd, k)
    to_senders = jnp.concatenate([jnp.where(domain_s == float(d), gd, 0.0) for d in range(9)], axis=0)
    to_receivers = jnp.concatenate([jnp.where(domain_r == float(d), gr, 0.0) for d in range(9)], axis=0)
    grads[...] = (
        put(split(to_senders), hot_s) - put(split(to_receivers), hot_r)
    ).reshape(9, 8, atoms)

    copies = []
    for d in others:
        copy = pltpu.make_async_remote_copy(
            src_ref=grads.at[d],
            dst_ref=back.at[8 - d],
            send_sem=send_b.at[d],
            recv_sem=recv_b.at[8 - d],
            device_id=neighbour(d),
            device_id_type=pl.DeviceIdType.MESH,
        )
        copy.start()
        copies.append(copy)
    for copy in copies:
        copy.wait()
    total = grads[4]
    for d in others:
        total = total + back[d]
    for k in range(3):
        out_ref[0, k] = -total[k : k + 1]


def part(both_ref, force_ref, energy_ref, sems):
    copies = [
        pltpu.make_async_copy(both_ref.at[:, 0:3], force_ref, sems.at[0]),
        pltpu.make_async_copy(both_ref.at[:, 3], energy_ref, sems.at[1]),
    ]
    for copy in copies:
        copy.start()
    for copy in copies:
        copy.wait()


def local(positions, species, senders, counts, owners, send_list, embedding,
          radial_in_one, radial_mid_one, radial_out_one, mixing, square_mix, readout_one,
          radial_in_two, radial_mid_two, radial_out_two, mix_two, read_hidden, read_out):
    atoms = positions.shape[3]
    layers = atoms // (SIDE * SIDE)
    slots, wide = senders.shape[2], 2 * atoms
    channels = embedding.shape[0]
    hidden, nbasis = radial_in_one.shape
    operands = (
        positions.transpose(0, 2, 1, 3), species, senders.transpose(0, 2, 1, 3), counts, send_list,
        owners.transpose(0, 2, 1, 3), embedding.T,
        radial_in_one.T, radial_mid_one, radial_out_one.T, mixing, square_mix, readout_one[None],
        radial_in_two.T, radial_mid_two, radial_out_two.T, mix_two, read_hidden, read_out[None],
    )
    vmem = pl.BlockSpec(memory_space=pltpu.VMEM)
    both = pl.pallas_call(
        functools.partial(kernel, layers),
        out_shape=jax.ShapeDtypeStruct((1, 4, 1, atoms), F32),
        in_specs=[pl.BlockSpec(memory_space=pltpu.HBM)] * len(operands),
        out_specs=vmem,
        scratch_shapes=[pltpu.VMEM(x.shape, x.dtype) for x in operands]
        + [
            pltpu.VMEM((9, ROWS, atoms), F32),
            pltpu.VMEM((9, 8, atoms), F32),
            pltpu.VMEM((9, 8, atoms), F32),
            pltpu.SemaphoreType.DMA((len(operands),)),
            pltpu.SemaphoreType.DMA((9,)),
            pltpu.SemaphoreType.DMA((9,)),
            pltpu.SemaphoreType.DMA((9,)),
            pltpu.SemaphoreType.DMA((9,)),
            pltpu.VMEM((slots, nbasis, wide), F32),
            pltpu.VMEM((slots, 8, wide), F32),
            pltpu.VMEM((slots, 8, wide), F32),
            pltpu.VMEM((slots, 2, hidden, wide), F32),
            pltpu.VMEM((slots, channels, wide), F32),
            pltpu.VMEM((slots, 3, channels, wide), F32),
            pltpu.VMEM((9, channels, wide), F32),
            pltpu.VMEM((9, channels, wide), F32),
            pltpu.VMEM((slots, nbasis, wide), F32),
            pltpu.VMEM((slots, 8, wide), F32),
        ],
        compiler_params=pltpu.CompilerParams(
            collective_id=0, has_side_effects=True, vmem_limit_bytes=64 * 1024 * 1024
        ),
    )(*operands)
    hbm = pl.BlockSpec(memory_space=pltpu.HBM)
    forces, energies = pl.pallas_call(
        part,
        out_shape=(
            jax.ShapeDtypeStruct(operands[0].shape, F32),
            jax.ShapeDtypeStruct(counts.shape, F32),
        ),
        in_specs=[hbm],
        out_specs=(hbm, hbm),
        scratch_shapes=[pltpu.SemaphoreType.DMA((2,))],
        compiler_params=pltpu.CompilerParams(vmem_limit_bytes=64 * 1024 * 1024),
    )(both)
    return forces.transpose(0, 2, 1, 3), energies


def solution(mesh):
    per_domain = (
        P("gx", "gy", None, None),
        P("gx", "gy", None),
        P("gx", "gy", None, None),
        P("gx", "gy", None),
        P("gx", "gy", None, None),
        P("gx", "gy", None),
    )
    return jax.shard_map(
        local,
        mesh=mesh,
        in_specs=per_domain + (P(),) * 13,
        out_specs=(P("gx", "gy", None, None), P("gx", "gy", None)),
        check_vma=False,
    )
```

```python
import functools
import math

import jax
import jax.numpy as jnp
from jax import lax
from jax.experimental import pallas as pl
from jax.experimental.pallas import tpu as pltpu
from jax.sharding import PartitionSpec as P

SIDE = 8
SPACING = 1.75
CUTOFF = 5.0
SOFTEN = 0.25
PAIR = 2.0
ROWS = 16
DEGREE = (0, 1, 1, 1, 2, 2, 2, 2, 2)
MEMBERS = ((0,), (1, 2, 3), (4, 5, 6, 7, 8))
F32 = jnp.float32
BF16 = jnp.bfloat16
NN = (((1,), (0,)), ((), ()))
NT = (((1,), (1,)), ((), ()))


def dot(a, b, dims=NN):
    return lax.dot_general(a, b, dims, preferred_element_type=F32)


def split(x):
    high = x.astype(BF16)
    return high, (x - high.astype(F32)).astype(BF16)


def split_three(x):
    high = x.astype(BF16)
    rest = x - high.astype(F32)
    return (high,) + split(rest)


def stack_left(x):
    high, low = split(x)
    high, low = high.astype(F32), low.astype(F32)
    return jnp.concatenate([high, low, high], axis=0).T.astype(BF16)


def left(x):
    high, low = split(x)
    return jnp.concatenate([high, low, high], axis=1)


def mm(left, b):
    high = b.astype(BF16).astype(F32)
    low = b - high
    if b.shape[0] % 16:
        right = jnp.concatenate([high, high, low], axis=0).astype(BF16)
    else:
        high, low = high.astype(BF16), low.astype(BF16)
        right = jnp.concatenate([high, high, low], axis=0)
    return dot(left, right)


def pick(parts, one_hot):
    return dot(jnp.concatenate(parts, axis=1), jnp.concatenate([one_hot] * len(parts), axis=0))


def put(parts, one_hot):
    return dot(jnp.concatenate(parts, axis=1), jnp.concatenate([one_hot] * len(parts), axis=1), NT)


def sin_cos_pi(t):
    turn = jnp.floor(t + 0.5)
    r = (t - turn) * math.pi
    sign = 1.0 - 2.0 * (turn - 2.0 * jnp.floor(turn * 0.5))
    z = r * r
    sine = jnp.full_like(z, 1.0 / math.factorial(13))
    cosine = jnp.full_like(z, -1.0 / math.factorial(14))
    for n in range(5, -1, -1):
        sine = sine * z + (-1.0) ** n / math.factorial(2 * n + 1)
    for n in range(6, -1, -1):
        cosine = cosine * z + (-1.0) ** n / math.factorial(2 * n)
    return sign * r * sine, sign * cosine


def floor_div(x, by):
    return jnp.floor((x + 0.5) * (1.0 / by))


def one_hot_rows(index, rows):
    ids = lax.broadcasted_iota(jnp.int32, (rows, index.shape[1]), 0).astype(F32)
    return jnp.where(ids == index, 1.0, 0.0).astype(BF16)


def by_domain(stacked, domain, rows):
    out = jnp.where(domain == 0.0, stacked[:rows], 0.0)
    for d in range(1, 9):
        out = out + jnp.where(domain == float(d), stacked[d * rows : (d + 1) * rows], 0.0)
    return out


def silu_pair(h):
    gate = 0.5 + 0.5 * jnp.tanh(0.5 * h)
    return h * gate, gate * (1.0 + h * (1.0 - gate))


def radial(basis, w_in, w_mid, w_out):
    s1, g1 = silu_pair(mm(w_in, basis))
    s2, g2 = silu_pair(mm(w_mid, s1))
    return mm(w_out, s2), g1, g2


def radial_back(g_out, w_in, w_mid, w_out, g1, g2):
    gh2 = mm(w_out, g_out) * g2
    gh1 = mm(w_mid, gh2) * g1
    return mm(w_in, gh1)


def kernel(
    layers,
    *refs,
):
    inputs, back, held = refs[:19], refs[19], refs[20:39]
    table, grads, load, send_a, recv_a, send_b, recv_b = refs[39:]
    (
        pos_ref, spec_ref, send_ref, cnt_ref, list_ref, own_ref, emb_ref,
        wi1_ref, wm1_ref, wo1_ref, mix_ref, sqm_ref, ro1_ref,
        wi2_ref, wm2_ref, wo2_ref, mx2_ref, rh_ref, ro2_ref,
    ) = held
    atoms = pos_ref.shape[3]
    bound = list_ref.shape[2]
    slots = send_ref.shape[1]
    species, channels = emb_ref.shape
    nbasis = wi1_ref.shape[0]
    column = SIDE * layers
    wide = 2 * atoms
    ring = (SIDE + 2) * layers
    used = (SIDE + 2) * ring
    me_x, me_y = lax.axis_index("gx"), lax.axis_index("gy")
    nx, ny = lax.axis_size("gx"), lax.axis_size("gy")

    def neighbour(d):
        return (lax.rem(me_x + (d // 3 - 1) + nx, nx), lax.rem(me_y + (d % 3 - 1) + ny, ny))

    others = [d for d in range(9) if d != 4]
    barrier = pltpu.get_barrier_semaphore()
    for d in others:
        pl.semaphore_signal(barrier, inc=1, device_id=neighbour(d), device_id_type=pl.DeviceIdType.MESH)

    loads = [pltpu.make_async_copy(inputs[i], held[i], load.at[i]) for i in range(19)]
    for copy in loads:
        copy.start()
    table[4] = jnp.zeros((ROWS, atoms), F32)
    for copy in loads[:5]:
        copy.wait()
    for k in range(3):
        table[4, k : k + 1, :] = pos_ref[0, k]
    table[4, 3:4, :] = spec_ref[0].astype(F32)
    for k in range(slots):
        table[4, 4 + k : 5 + k, :] = send_ref[0, k].astype(F32)
    table[4, 7:8, :] = cnt_ref[0].astype(F32)
    table[4, 8:9, 0:bound] = list_ref[0].astype(F32)
    pl.semaphore_wait(barrier, 8)
    copies = []
    for d in others:
        copy = pltpu.make_async_remote_copy(
            src_ref=table.at[4],
            dst_ref=table.at[8 - d],
            send_sem=send_a.at[d],
            recv_sem=recv_a.at[8 - d],
            device_id=neighbour(d),
            device_id_type=pl.DeviceIdType.MESH,
        )
        copy.start()
        copies.append(copy)

    lane = lax.broadcasted_iota(jnp.int32, (1, wide), 1).astype(F32)
    ring_at = lane - atoms
    low_x = ring_at < ring
    long_side = ring_at < 2 * ring
    along = jnp.where(low_x, ring_at, ring_at - ring)
    in_y = ring_at - 2 * ring
    low_y = in_y < column
    across = jnp.where(low_y, in_y, in_y - column)
    half_long = floor_div(along, layers)
    half_short = floor_div(across, layers)
    site_x = jnp.where(long_side, jnp.where(low_x, -1.0, float(SIDE)), half_short)
    site_y = jnp.where(long_side, half_long - 1.0, jnp.where(low_y, -1.0, float(SIDE)))
    site_z = jnp.where(long_side, along - half_long * layers, across - half_short * layers)
    inside = (lane < atoms) | (lane >= used)
    off_x = jnp.where(inside, 0.0, floor_div(site_x, SIDE))
    off_y = jnp.where(inside, 0.0, floor_div(site_y, SIDE))
    ring_atom = (site_x - off_x * SIDE) * column + (site_y - off_y * SIDE) * layers + site_z
    atom_r = jnp.where(lane < atoms, lane, jnp.where(lane >= used, 0.0, ring_atom))
    domain_r = 3.0 * (off_x + 1.0) + (off_y + 1.0)
    hot_r = one_hot_rows(atom_r, atoms)

    for copy in loads[5:]:
        copy.wait()
    wi1, wi1_back = stack_left(wi1_ref[...]), stack_left(wi1_ref[...].T)
    wi2, wi2_back = stack_left(wi2_ref[...]), stack_left(wi2_ref[...].T)
    wm1, wm1_back = stack_left(wm1_ref[...].T), stack_left(wm1_ref[...])
    wm2, wm2_back = stack_left(wm2_ref[...].T), stack_left(wm2_ref[...])
    wo1, wo1_back = stack_left(wo1_ref[...]), left(wo1_ref[...])
    wo2, wo2_back = stack_left(wo2_ref[...]), left(wo2_ref[...])
    mix = [left(mix_ref[l]) for l in range(3)]
    mix_back = [left(mix_ref[l].T) for l in range(3)]
    sqm, sqm_back = left(sqm_ref[...]), left(sqm_ref[...].T)
    rh, rh_back = left(rh_ref[...]), stack_left(rh_ref[...])
    joined = mm(rh, mx2_ref[...])
    both, both_back = left(joined), stack_left(joined)
    emb = split_three(emb_ref[...].T)
    ro1_cols = jnp.broadcast_to(ro1_ref[...], (atoms, channels)).T
    ro2_cols = jnp.broadcast_to(ro2_ref[...], (atoms, ro2_ref.shape[1])).T

    for copy in copies:
        copy.wait()

    def tile(x):
        return jnp.concatenate([x] * slots, axis=1)

    def slot(x, k):
        return x[:, k * wide : (k + 1) * wide]

    def own(x):
        return jnp.concatenate([x[:, k * wide : k * wide + atoms] for k in range(slots)], axis=1)

    def own_slot(x, k):
        return x[:, k * atoms : (k + 1) * atoms]

    def spread(x):
        zero = jnp.zeros((x.shape[0], atoms), F32)
        return jnp.concatenate([p for k in range(slots) for p in (own_slot(x, k), zero)], axis=1)

    everything = table[...].reshape(9 * ROWS, atoms)
    parts = split_three(everything)
    rec = by_domain(pick(parts, hot_r), domain_r, ROWS)
    sender = jnp.concatenate([rec[4 + k : 5 + k] for k in range(slots)], axis=1)
    live = jnp.concatenate(
        [jnp.where((rec[7:8] > float(k)) & (lane < used), 1.0, 0.0) for k in range(slots)], axis=1
    )
    is_local = sender < atoms
    ghost = sender - atoms
    block = floor_div(ghost, bound)
    place = ghost - block * bound
    block = jnp.where(block >= 4.0, block + 1.0, block)
    block = jnp.where(is_local, 4.0, block)
    block_x = floor_div(block, 3)
    block_y = block - 3.0 * block_x - 1.0
    block_x = block_x - 1.0
    to_x = tile(off_x) + block_x
    to_y = tile(off_y) + block_y
    domain_s = 3.0 * (to_x + 1.0) + (to_y + 1.0)
    lists = dot(parts[0], one_hot_rows(place, atoms))
    listed = jnp.zeros_like(sender)
    for d in range(9):
        listed = listed + jnp.where(domain_s == float(d), lists[d * ROWS + 8 : d * ROWS + 9], 0.0)
    atom_s = jnp.where(is_local, sender, listed)
    hot_s = one_hot_rows(atom_s, atoms)
    upper = jnp.concatenate([table[d, 0:8, :] for d in range(9)], axis=0)
    snd = by_domain(pick(split_three(upper), hot_s), domain_s, 8)

    side_length = SPACING * SIDE
    dx = (snd[0:1] + block_x * side_length) - tile(rec[0:1])
    dy = (snd[1:2] + block_y * side_length) - tile(rec[1:2])
    dz = snd[2:3] - tile(rec[2:3])
    radius = jnp.sqrt(dx * dx + dy * dy + dz * dz + SOFTEN)
    inverse = 1.0 / radius
    ux, uy, uz = dx * inverse, dy * inverse, dz * inverse
    x = jnp.minimum(radius / CUTOFF, 1.0)
    x2 = x * x
    x5 = x2 * x2 * x
    x6 = x5 * x
    envelope = 1.0 + x6 * (-28.0 + x * (48.0 - 21.0 * x))
    slope = jnp.where(radius < CUTOFF, 1.0 / CUTOFF, 0.0)
    d_envelope = x5 * (-168.0 + x * (336.0 - 168.0 * x)) * slope
    orders = (lax.broadcasted_iota(jnp.int32, (nbasis, 1), 0) + 1).astype(F32)
    scale = math.sqrt(2.0 / CUTOFF)
    sines, cosines = sin_cos_pi(orders * x)
    sines = sines * scale
    cosines = cosines * (orders * (scale * math.pi))
    basis = sines * (inverse * envelope)
    d_basis = cosines * (slope * inverse * envelope) + sines * (
        inverse * d_envelope - inverse * inverse * envelope
    )
    r3, r5, r15 = math.sqrt(3.0), math.sqrt(5.0), math.sqrt(15.0)
    shapes = [
        None,
        r3 * ux,
        r3 * uy,
        r3 * uz,
        r15 * ux * uy,
        r15 * uy * uz,
        0.5 * r5 * (2.0 * uz * uz - ux * ux - uy * uy),
        r15 * ux * uz,
        0.5 * r15 * (ux * ux - uy * uy),
    ]

    def rows_of(w, l):
        return w[l * channels : (l + 1) * channels]

    species_row = lax.broadcasted_iota(jnp.int32, (species, 1), 0).astype(F32)
    hot_es = jnp.where(species_row == snd[3:4], 1.0, 0.0).astype(BF16)
    hot_er = jnp.where(species_row == rec[3:4], 1.0, 0.0).astype(BF16)
    carrier = pick(emb, hot_es) * (live * (1.0 / slots))
    embedded = pick(emb, hot_er)
    edge_one, one_g1, one_g2 = radial(basis, wi1, wm1, wo1)
    carried = [rows_of(edge_one, l) * carrier for l in range(3)]
    moments = []
    for m in range(9):
        term = carried[DEGREE[m]] if m == 0 else carried[DEGREE[m]] * shapes[m]
        total = slot(term, 0)
        for k in range(1, slots):
            total = total + slot(term, k)
        moments.append(total)
    squares = moments[0] * moments[0]
    for m in range(1, 9):
        squares = squares + moments[m] * moments[m]
    features = [mm(mix[0], moments[0]) + mm(sqm, squares) + embedded]
    for l in (1, 2):
        mixed = mm(mix[l], jnp.concatenate([moments[m] for m in MEMBERS[l]], axis=1))
        features += [mixed[:, i * wide : (i + 1) * wide] for i in range(len(MEMBERS[l]))]

    live_two = own(live) * (1.0 / slots)
    edge_two, two_g1, two_g2 = radial(own(basis), wi2, wm2, wo2)
    shapes_two = [None] + [own(s) for s in shapes[1:]]
    at_two, to_x2, to_y2 = own(atom_s), own(to_x), own(to_y)
    ax = floor_div(at_two, column)
    rest = at_two - ax * column
    ay = floor_div(rest, layers)
    az = rest - ay * layers
    sx = ax + to_x2 * SIDE
    sy = ay + to_y2 * SIDE
    outside = jnp.where(
        to_x2 != 0.0,
        jnp.where(to_x2 < 0.0, 0.0, float(ring)) + (sy + 1.0) * layers + az,
        2.0 * ring + jnp.where(to_y2 < 0.0, 0.0, float(column)) + sx * layers + az,
    )
    at_ring = jnp.where((to_x2 == 0.0) & (to_y2 == 0.0), at_two, atoms + outside)
    hot_two = one_hot_rows(at_ring, wide)
    stacked = jnp.concatenate(features, axis=0)
    sent = pick(split(stacked), hot_two)
    projected = []
    for l in range(3):
        total = None
        for m in MEMBERS[l]:
            term = rows_of(sent, m) if m == 0 else rows_of(sent, m) * shapes_two[m]
            total = term if total is None else total + term
        projected.append(total)
    scalar = sum(rows_of(edge_two, l) * projected[l] for l in range(3)) * live_two
    gathered = own_slot(scalar, 0)
    for k in range(1, slots):
        gathered = gathered + own_slot(scalar, k)
    hidden, hidden_slope = silu_pair(mm(both, gathered) + mm(rh, features[0][:, :atoms]))
    energy_two = jnp.sum(ro2_cols * hidden, axis=0, keepdims=True)
    energy_one = jnp.sum(ro1_cols * features[0][:, :atoms], axis=0, keepdims=True)
    owners = jnp.concatenate([own_ref[0, k].astype(F32) for k in range(slots)], axis=1)
    decay = PAIR * jnp.exp(-own(radius)) * owners * own(live)
    pair = decay * own(envelope)
    energy = energy_one + energy_two
    for k in range(slots):
        energy = energy + own_slot(pair, k)
    g_radius_pair = decay * (own(d_envelope) - own(envelope))

    g_hidden = ro2_cols * hidden_slope
    g_refined = mm(rh_back, g_hidden)
    g_gathered = mm(both_back, g_hidden)
    t = jnp.concatenate([g_gathered] * slots, axis=1) * live_two
    g_edge_two = jnp.concatenate([t * projected[l] for l in range(3)], axis=0)
    g_proj = [t * rows_of(edge_two, l) for l in range(3)]
    g_sent = jnp.concatenate(
        [g_proj[0]] + [g_proj[DEGREE[m]] * shapes_two[m] for m in range(1, 9)], axis=0
    )
    g_shapes_two = [
        jnp.sum(g_proj[DEGREE[m]] * rows_of(sent, m), axis=0, keepdims=True) for m in range(1, 9)
    ]
    g_basis_two = radial_back(g_edge_two, wi2_back, wm2_back, wo2_back, two_g1, two_g2)
    g_stacked = put(split(g_sent), hot_two)
    g_features = [rows_of(g_stacked, m) for m in range(9)]
    g_features[0] = g_features[0] + jnp.concatenate(
        [g_refined + ro1_cols, jnp.zeros((channels, wide - atoms), F32)], axis=1
    )

    g_squares = mm(sqm_back, g_features[0]) * 2.0
    g_moments = [mm(mix_back[0], g_features[0])]
    for l in (1, 2):
        mixed = mm(mix_back[l], jnp.concatenate([g_features[m] for m in MEMBERS[l]], axis=1))
        g_moments += [mixed[:, i * wide : (i + 1) * wide] for i in range(len(MEMBERS[l]))]
    g_moments = [g + g_squares * moments[m] for m, g in enumerate(g_moments)]
    g_edge_one = []
    g_shapes = []
    for l in range(3):
        total = None
        for m in MEMBERS[l]:
            tiled = tile(g_moments[m])
            term = tiled if m == 0 else tiled * shapes[m]
            total = term if total is None else total + term
            if m > 0:
                g_shapes.append(jnp.sum(tiled * carried[l], axis=0, keepdims=True))
        g_edge_one.append(total * carrier)
    g_basis = radial_back(
        jnp.concatenate(g_edge_one, axis=0), wi1_back, wm1_back, wo1_back, one_g1, one_g2
    )

    g_basis = g_basis + spread(g_basis_two)
    g = [None] + [g_shapes[m] + spread(g_shapes_two[m]) for m in range(8)]
    g_radius = jnp.sum(g_basis * d_basis, axis=0, keepdims=True) + spread(g_radius_pair)
    gux = r3 * g[1] + r15 * (g[4] * uy + g[7] * uz + g[8] * ux) - r5 * ux * g[6]
    guy = r3 * g[2] + r15 * (g[4] * ux + g[5] * uz - g[8] * uy) - r5 * uy * g[6]
    guz = r3 * g[3] + r15 * (g[5] * uy + g[7] * ux) + 2.0 * r5 * uz * g[6]
    radial_part = g_radius - inverse * (gux * ux + guy * uy + guz * uz)
    gd = [inverse * gu + u * radial_part for gu, u in ((gux, ux), (guy, uy), (guz, uz))]
    gd = jnp.concatenate(gd + [jnp.zeros((5, gd[0].shape[1]), F32)], axis=0)
    gr = slot(gd, 0)
    for k in range(1, slots):
        gr = gr + slot(gd, k)
    to_senders = jnp.concatenate([jnp.where(domain_s == float(d), gd, 0.0) for d in range(9)], axis=0)
    to_receivers = jnp.concatenate([jnp.where(domain_r == float(d), gr, 0.0) for d in range(9)], axis=0)
    grads[...] = (
        put(split(to_senders), hot_s) - put(split(to_receivers), hot_r)
    ).reshape(9, 8, atoms)
    copies = []
    for d in others:
        copy = pltpu.make_async_remote_copy(
            src_ref=grads.at[d],
            dst_ref=back.at[8 - d],
            send_sem=send_b.at[d],
            recv_sem=recv_b.at[8 - d],
            device_id=neighbour(d),
            device_id_type=pl.DeviceIdType.MESH,
        )
        copy.start()
        copies.append(copy)
    grads[4, 3:4, :] = energy
    copy = pltpu.make_async_copy(grads.at[4], back.at[4], send_b.at[4])
    copy.start()
    for copy in copies + [copy]:
        copy.wait()


def settle(back_ref, force_ref, energy_ref):
    total = back_ref[0]
    for d in range(1, 9):
        total = total + back_ref[d]
    for k in range(3):
        force_ref[0, k] = -total[k : k + 1]
    energy_ref[0] = back_ref[4, 3:4, :]


def local(positions, species, senders, counts, owners, send_list, embedding,
          radial_in_one, radial_mid_one, radial_out_one, mixing, square_mix, readout_one,
          radial_in_two, radial_mid_two, radial_out_two, mix_two, read_hidden, read_out):
    atoms = positions.shape[3]
    layers = atoms // (SIDE * SIDE)
    operands = (
        positions.transpose(0, 2, 1, 3), species, senders.transpose(0, 2, 1, 3), counts, send_list,
        owners.transpose(0, 2, 1, 3), embedding.T,
        radial_in_one.T, radial_mid_one, radial_out_one.T, mixing, square_mix, readout_one[None],
        radial_in_two.T, radial_mid_two, radial_out_two.T, mix_two, read_hidden, read_out[None],
    )
    vmem = pl.BlockSpec(memory_space=pltpu.VMEM)
    hbm = pl.BlockSpec(memory_space=pltpu.HBM)
    back = pl.pallas_call(
        functools.partial(kernel, layers),
        out_shape=jax.ShapeDtypeStruct((9, 8, atoms), F32),
        in_specs=[hbm] * len(operands),
        out_specs=hbm,
        scratch_shapes=[pltpu.VMEM(x.shape, x.dtype) for x in operands]
        + [
            pltpu.VMEM((9, ROWS, atoms), F32),
            pltpu.VMEM((9, 8, atoms), F32),
            pltpu.SemaphoreType.DMA((len(operands),)),
            pltpu.SemaphoreType.DMA((9,)),
            pltpu.SemaphoreType.DMA((9,)),
            pltpu.SemaphoreType.DMA((9,)),
            pltpu.SemaphoreType.DMA((9,)),
        ],
        compiler_params=pltpu.CompilerParams(
            collective_id=0, has_side_effects=True, vmem_limit_bytes=64 * 1024 * 1024
        ),
    )(*operands)
    forces, energies = pl.pallas_call(
        settle,
        out_shape=(
            jax.ShapeDtypeStruct(operands[0].shape, F32),
            jax.ShapeDtypeStruct(counts.shape, F32),
        ),
        in_specs=[vmem],
        out_specs=(vmem, vmem),
        compiler_params=pltpu.CompilerParams(vmem_limit_bytes=64 * 1024 * 1024),
    )(back)
    return forces.transpose(0, 2, 1, 3), energies


def solution(mesh):
    per_domain = (
        P("gx", "gy", None, None),
        P("gx", "gy", None),
        P("gx", "gy", None, None),
        P("gx", "gy", None),
        P("gx", "gy", None, None),
        P("gx", "gy", None),
    )
    return jax.shard_map(
        local,
        mesh=mesh,
        in_specs=per_domain + (P(),) * 13,
        out_specs=(P("gx", "gy", None, None), P("gx", "gy", None)),
        check_vma=False,
    )
```

```python
import functools
import math

import jax
import jax.numpy as jnp
from jax import lax
from jax.experimental import pallas as pl
from jax.experimental.pallas import tpu as pltpu
from jax.sharding import PartitionSpec as P

SIDE = 8
SPACING = 1.75
CUTOFF = 5.0
SOFTEN = 0.25
PAIR = 2.0
ROWS = 16
DEGREE = (0, 1, 1, 1, 2, 2, 2, 2, 2)
MEMBERS = ((0,), (1, 2, 3), (4, 5, 6, 7, 8))
F32 = jnp.float32
BF16 = jnp.bfloat16
NN = (((1,), (0,)), ((), ()))
NT = (((1,), (1,)), ((), ()))


def dot(a, b, dims=NN):
    return lax.dot_general(a, b, dims, preferred_element_type=F32)


def split(x):
    high = x.astype(BF16)
    return high, (x - high.astype(F32)).astype(BF16)


def split_three(x):
    high = x.astype(BF16)
    rest = x - high.astype(F32)
    return (high,) + split(rest)


def stack_left(x):
    high, low = split(x)
    high, low = high.astype(F32), low.astype(F32)
    return jnp.concatenate([high, low, high], axis=0).T.astype(BF16)


def left(x):
    high, low = split(x)
    lower = jnp.concatenate([low, jnp.zeros_like(low)], axis=1)
    return jnp.concatenate([jnp.concatenate([high, high], axis=1), lower], axis=0)


def mm_rows(left, b):
    out = dot(left, jnp.concatenate(split(b), axis=0))
    half = left.shape[0] // 2
    return out[:half] + out[half:]


def mm(left, b):
    high = b.astype(BF16).astype(F32)
    low = b - high
    if b.shape[0] % 16:
        right = jnp.concatenate([high, high, low], axis=0).astype(BF16)
    else:
        high, low = high.astype(BF16), low.astype(BF16)
        right = jnp.concatenate([high, high, low], axis=0)
    return dot(left, right)


def pick(parts, one_hot):
    return dot(jnp.concatenate(parts, axis=1), jnp.concatenate([one_hot] * len(parts), axis=0))


def put(parts, one_hot):
    return dot(jnp.concatenate(parts, axis=1), jnp.concatenate([one_hot] * len(parts), axis=1), NT)


def sin_cos_pi(t):
    turn = jnp.floor(t + 0.5)
    r = (t - turn) * math.pi
    sign = 1.0 - 2.0 * (turn - 2.0 * jnp.floor(turn * 0.5))
    z = r * r
    sine = jnp.full_like(z, 1.0 / math.factorial(13))
    cosine = jnp.full_like(z, -1.0 / math.factorial(14))
    for n in range(5, -1, -1):
        sine = sine * z + (-1.0) ** n / math.factorial(2 * n + 1)
    for n in range(6, -1, -1):
        cosine = cosine * z + (-1.0) ** n / math.factorial(2 * n)
    return sign * r * sine, sign * cosine


def floor_div(x, by):
    return jnp.floor((x + 0.5) * (1.0 / by))


def one_hot_rows(index, rows):
    ids = lax.broadcasted_iota(jnp.int32, (rows, index.shape[1]), 0).astype(F32)
    return jnp.where(ids == index, 1.0, 0.0).astype(BF16)


def by_domain(stacked, domain, rows):
    out = jnp.where(domain == 0.0, stacked[:rows], 0.0)
    for d in range(1, 9):
        out = out + jnp.where(domain == float(d), stacked[d * rows : (d + 1) * rows], 0.0)
    return out


def silu_pair(h):
    gate = 0.5 + 0.5 * jnp.tanh(0.5 * h)
    return h * gate, gate * (1.0 + h * (1.0 - gate))


def radial(basis, w_in, w_mid, w_out):
    s1, g1 = silu_pair(mm(w_in, basis))
    s2, g2 = silu_pair(mm(w_mid, s1))
    return mm(w_out, s2), g1, g2


def radial_back(g_out, w_in, w_mid, w_out, g1, g2):
    gh2 = mm_rows(w_out, g_out) * g2
    gh1 = mm(w_mid, gh2) * g1
    return mm(w_in, gh1)


def kernel(
    layers,
    *refs,
):
    inputs, back, held = refs[:19], refs[19], refs[20:39]
    table, grads, load, send_a, recv_a, send_b, recv_b = refs[39:]
    (
        pos_ref, spec_ref, send_ref, cnt_ref, list_ref, own_ref, emb_ref,
        wi1_ref, wm1_ref, wo1_ref, mix_ref, sqm_ref, ro1_ref,
        wi2_ref, wm2_ref, wo2_ref, mx2_ref, rh_ref, ro2_ref,
    ) = held
    atoms = pos_ref.shape[3]
    bound = list_ref.shape[2]
    slots = send_ref.shape[1]
    species, channels = emb_ref.shape
    nbasis = wi1_ref.shape[0]
    column = SIDE * layers
    wide = 2 * atoms
    ring = (SIDE + 2) * layers
    used = (SIDE + 2) * ring
    me_x, me_y = lax.axis_index("gx"), lax.axis_index("gy")
    nx, ny = lax.axis_size("gx"), lax.axis_size("gy")

    def neighbour(d):
        return (lax.rem(me_x + (d // 3 - 1) + nx, nx), lax.rem(me_y + (d % 3 - 1) + ny, ny))

    others = [d for d in range(9) if d != 4]
    barrier = pltpu.get_barrier_semaphore()
    for d in others:
        pl.semaphore_signal(barrier, inc=1, device_id=neighbour(d), device_id_type=pl.DeviceIdType.MESH)

    loads = [pltpu.make_async_copy(inputs[i], held[i], load.at[i]) for i in range(19)]
    for copy in loads:
        copy.start()
    table[4] = jnp.zeros((ROWS, atoms), F32)
    for copy in loads[:5]:
        copy.wait()
    for k in range(3):
        table[4, k : k + 1, :] = pos_ref[0, k]
    table[4, 3:4, :] = spec_ref[0].astype(F32)
    for k in range(slots):
        table[4, 4 + k : 5 + k, :] = send_ref[0, k].astype(F32)
    table[4, 7:8, :] = cnt_ref[0].astype(F32)
    table[4, 8:9, 0:bound] = list_ref[0].astype(F32)
    pl.semaphore_wait(barrier, 8)
    copies = []
    for d in others:
        copy = pltpu.make_async_remote_copy(
            src_ref=table.at[4],
            dst_ref=table.at[8 - d],
            send_sem=send_a.at[d],
            recv_sem=recv_a.at[8 - d],
            device_id=neighbour(d),
            device_id_type=pl.DeviceIdType.MESH,
        )
        copy.start()
        copies.append(copy)

    lane = lax.broadcasted_iota(jnp.int32, (1, wide), 1).astype(F32)
    ring_at = lane - atoms
    low_x = ring_at < ring
    long_side = ring_at < 2 * ring
    along = jnp.where(low_x, ring_at, ring_at - ring)
    in_y = ring_at - 2 * ring
    low_y = in_y < column
    across = jnp.where(low_y, in_y, in_y - column)
    half_long = floor_div(along, layers)
    half_short = floor_div(across, layers)
    site_x = jnp.where(long_side, jnp.where(low_x, -1.0, float(SIDE)), half_short)
    site_y = jnp.where(long_side, half_long - 1.0, jnp.where(low_y, -1.0, float(SIDE)))
    site_z = jnp.where(long_side, along - half_long * layers, across - half_short * layers)
    inside = (lane < atoms) | (lane >= used)
    off_x = jnp.where(inside, 0.0, floor_div(site_x, SIDE))
    off_y = jnp.where(inside, 0.0, floor_div(site_y, SIDE))
    ring_atom = (site_x - off_x * SIDE) * column + (site_y - off_y * SIDE) * layers + site_z
    atom_r = jnp.where(lane < atoms, lane, jnp.where(lane >= used, 0.0, ring_atom))
    domain_r = 3.0 * (off_x + 1.0) + (off_y + 1.0)
    hot_r = one_hot_rows(atom_r, atoms)

    for copy in loads[5:]:
        copy.wait()
    wi1, wi1_back = stack_left(wi1_ref[...]), stack_left(wi1_ref[...].T)
    wi2, wi2_back = stack_left(wi2_ref[...]), stack_left(wi2_ref[...].T)
    wm1, wm1_back = stack_left(wm1_ref[...].T), stack_left(wm1_ref[...])
    wm2, wm2_back = stack_left(wm2_ref[...].T), stack_left(wm2_ref[...])
    wo1, wo1_back = stack_left(wo1_ref[...]), left(wo1_ref[...])
    wo2, wo2_back = stack_left(wo2_ref[...]), left(wo2_ref[...])
    mix = [left(mix_ref[l]) for l in range(3)]
    mix_back = [left(mix_ref[l].T) for l in range(3)]
    sqm, sqm_back = left(sqm_ref[...]), left(sqm_ref[...].T)
    rh, rh_back = left(rh_ref[...]), stack_left(rh_ref[...])
    joined = mm_rows(rh, mx2_ref[...])
    both, both_back = left(joined), stack_left(joined)
    emb = split_three(emb_ref[...].T)
    ro1_cols = jnp.broadcast_to(ro1_ref[...], (atoms, channels)).T
    ro2_cols = jnp.broadcast_to(ro2_ref[...], (atoms, ro2_ref.shape[1])).T

    for copy in copies:
        copy.wait()

    def tile(x):
        return jnp.concatenate([x] * slots, axis=1)

    def slot(x, k):
        return x[:, k * wide : (k + 1) * wide]

    def own(x):
        return jnp.concatenate([x[:, k * wide : k * wide + atoms] for k in range(slots)], axis=1)

    def own_slot(x, k):
        return x[:, k * atoms : (k + 1) * atoms]

    def spread(x):
        zero = jnp.zeros((x.shape[0], atoms), F32)
        return jnp.concatenate([p for k in range(slots) for p in (own_slot(x, k), zero)], axis=1)

    everything = table[...].reshape(9 * ROWS, atoms)
    parts = split_three(everything)
    rec = by_domain(pick(parts, hot_r), domain_r, ROWS)
    sender = jnp.concatenate([rec[4 + k : 5 + k] for k in range(slots)], axis=1)
    live = jnp.concatenate(
        [jnp.where((rec[7:8] > float(k)) & (lane < used), 1.0, 0.0) for k in range(slots)], axis=1
    )
    is_local = sender < atoms
    ghost = sender - atoms
    block = floor_div(ghost, bound)
    place = ghost - block * bound
    block = jnp.where(block >= 4.0, block + 1.0, block)
    block = jnp.where(is_local, 4.0, block)
    block_x = floor_div(block, 3)
    block_y = block - 3.0 * block_x - 1.0
    block_x = block_x - 1.0
    to_x = tile(off_x) + block_x
    to_y = tile(off_y) + block_y
    domain_s = 3.0 * (to_x + 1.0) + (to_y + 1.0)
    lists = dot(parts[0], one_hot_rows(place, atoms))
    listed = jnp.zeros_like(sender)
    for d in range(9):
        listed = listed + jnp.where(domain_s == float(d), lists[d * ROWS + 8 : d * ROWS + 9], 0.0)
    atom_s = jnp.where(is_local, sender, listed)
    hot_s = one_hot_rows(atom_s, atoms)
    upper = jnp.concatenate([table[d, 0:8, :] for d in range(9)], axis=0)
    snd = by_domain(pick(split_three(upper), hot_s), domain_s, 8)

    side_length = SPACING * SIDE
    dx = (snd[0:1] + block_x * side_length) - tile(rec[0:1])
    dy = (snd[1:2] + block_y * side_length) - tile(rec[1:2])
    dz = snd[2:3] - tile(rec[2:3])
    radius = jnp.sqrt(dx * dx + dy * dy + dz * dz + SOFTEN)
    inverse = 1.0 / radius
    ux, uy, uz = dx * inverse, dy * inverse, dz * inverse
    x = jnp.minimum(radius / CUTOFF, 1.0)
    x2 = x * x
    x5 = x2 * x2 * x
    x6 = x5 * x
    envelope = 1.0 + x6 * (-28.0 + x * (48.0 - 21.0 * x))
    slope = jnp.where(radius < CUTOFF, 1.0 / CUTOFF, 0.0)
    d_envelope = x5 * (-168.0 + x * (336.0 - 168.0 * x)) * slope
    orders = (lax.broadcasted_iota(jnp.int32, (nbasis, 1), 0) + 1).astype(F32)
    scale = math.sqrt(2.0 / CUTOFF)
    sines, cosines = sin_cos_pi(orders * x)
    sines = sines * scale
    cosines = cosines * (orders * (scale * math.pi))
    basis = sines * (inverse * envelope)
    d_basis = cosines * (slope * inverse * envelope) + sines * (
        inverse * d_envelope - inverse * inverse * envelope
    )
    r3, r5, r15 = math.sqrt(3.0), math.sqrt(5.0), math.sqrt(15.0)
    shapes = [
        None,
        r3 * ux,
        r3 * uy,
        r3 * uz,
        r15 * ux * uy,
        r15 * uy * uz,
        0.5 * r5 * (2.0 * uz * uz - ux * ux - uy * uy),
        r15 * ux * uz,
        0.5 * r15 * (ux * ux - uy * uy),
    ]

    def rows_of(w, l):
        return w[l * channels : (l + 1) * channels]

    species_row = lax.broadcasted_iota(jnp.int32, (species, 1), 0).astype(F32)
    hot_es = jnp.where(species_row == snd[3:4], 1.0, 0.0).astype(BF16)
    hot_er = jnp.where(species_row == rec[3:4], 1.0, 0.0).astype(BF16)
    carrier = pick(emb, hot_es) * (live * (1.0 / slots))
    embedded = pick(emb, hot_er)
    edge_one, one_g1, one_g2 = radial(basis, wi1, wm1, wo1)
    carried = [rows_of(edge_one, l) * carrier for l in range(3)]
    moments = []
    for m in range(9):
        term = carried[DEGREE[m]] if m == 0 else carried[DEGREE[m]] * shapes[m]
        total = slot(term, 0)
        for k in range(1, slots):
            total = total + slot(term, k)
        moments.append(total)
    squares = moments[0] * moments[0]
    for m in range(1, 9):
        squares = squares + moments[m] * moments[m]
    features = [mm_rows(mix[0], moments[0]) + mm_rows(sqm, squares) + embedded]
    for l in (1, 2):
        mixed = mm_rows(mix[l], jnp.concatenate([moments[m] for m in MEMBERS[l]], axis=1))
        features += [mixed[:, i * wide : (i + 1) * wide] for i in range(len(MEMBERS[l]))]

    live_two = own(live) * (1.0 / slots)
    edge_two, two_g1, two_g2 = radial(own(basis), wi2, wm2, wo2)
    shapes_two = [None] + [own(s) for s in shapes[1:]]
    at_two, to_x2, to_y2 = own(atom_s), own(to_x), own(to_y)
    ax = floor_div(at_two, column)
    rest = at_two - ax * column
    ay = floor_div(rest, layers)
    az = rest - ay * layers
    sx = ax + to_x2 * SIDE
    sy = ay + to_y2 * SIDE
    outside = jnp.where(
        to_x2 != 0.0,
        jnp.where(to_x2 < 0.0, 0.0, float(ring)) + (sy + 1.0) * layers + az,
        2.0 * ring + jnp.where(to_y2 < 0.0, 0.0, float(column)) + sx * layers + az,
    )
    at_ring = jnp.where((to_x2 == 0.0) & (to_y2 == 0.0), at_two, atoms + outside)
    hot_two = one_hot_rows(at_ring, wide)
    stacked = jnp.concatenate(features, axis=0)
    sent = pick(split(stacked), hot_two)
    projected = []
    for l in range(3):
        total = None
        for m in MEMBERS[l]:
            term = rows_of(sent, m) if m == 0 else rows_of(sent, m) * shapes_two[m]
            total = term if total is None else total + term
        projected.append(total)
    scalar = sum(rows_of(edge_two, l) * projected[l] for l in range(3)) * live_two
    gathered = own_slot(scalar, 0)
    for k in range(1, slots):
        gathered = gathered + own_slot(scalar, k)
    hidden, hidden_slope = silu_pair(mm_rows(both, gathered) + mm_rows(rh, features[0][:, :atoms]))
    energy_two = jnp.sum(ro2_cols * hidden, axis=0, keepdims=True)
    energy_one = jnp.sum(ro1_cols * features[0][:, :atoms], axis=0, keepdims=True)
    owners = jnp.concatenate([own_ref[0, k].astype(F32) for k in range(slots)], axis=1)
    decay = PAIR * jnp.exp(-own(radius)) * owners * own(live)
    pair = decay * own(envelope)
    energy = energy_one + energy_two
    for k in range(slots):
        energy = energy + own_slot(pair, k)
    g_radius_pair = decay * (own(d_envelope) - own(envelope))

    g_hidden = ro2_cols * hidden_slope
    g_refined = mm(rh_back, g_hidden)
    g_gathered = mm(both_back, g_hidden)
    t = jnp.concatenate([g_gathered] * slots, axis=1) * live_two
    g_edge_two = jnp.concatenate([t * projected[l] for l in range(3)], axis=0)
    g_proj = [t * rows_of(edge_two, l) for l in range(3)]
    g_sent = jnp.concatenate(
        [g_proj[0]] + [g_proj[DEGREE[m]] * shapes_two[m] for m in range(1, 9)], axis=0
    )
    g_shapes_two = [
        jnp.sum(g_proj[DEGREE[m]] * rows_of(sent, m), axis=0, keepdims=True) for m in range(1, 9)
    ]
    g_basis_two = radial_back(g_edge_two, wi2_back, wm2_back, wo2_back, two_g1, two_g2)
    g_stacked = put(split(g_sent), hot_two)
    g_features = [rows_of(g_stacked, m) for m in range(9)]
    g_features[0] = g_features[0] + jnp.concatenate(
        [g_refined + ro1_cols, jnp.zeros((channels, wide - atoms), F32)], axis=1
    )

    g_squares = mm_rows(sqm_back, g_features[0]) * 2.0
    g_moments = [mm_rows(mix_back[0], g_features[0])]
    for l in (1, 2):
        mixed = mm_rows(mix_back[l], jnp.concatenate([g_features[m] for m in MEMBERS[l]], axis=1))
        g_moments += [mixed[:, i * wide : (i + 1) * wide] for i in range(len(MEMBERS[l]))]
    g_moments = [g + g_squares * moments[m] for m, g in enumerate(g_moments)]
    g_edge_one = []
    g_shapes = []
    for l in range(3):
        total = None
        for m in MEMBERS[l]:
            tiled = tile(g_moments[m])
            term = tiled if m == 0 else tiled * shapes[m]
            total = term if total is None else total + term
            if m > 0:
                g_shapes.append(jnp.sum(tiled * carried[l], axis=0, keepdims=True))
        g_edge_one.append(total * carrier)
    g_basis = radial_back(
        jnp.concatenate(g_edge_one, axis=0), wi1_back, wm1_back, wo1_back, one_g1, one_g2
    )

    g_basis = g_basis + spread(g_basis_two)
    g = [None] + [g_shapes[m] + spread(g_shapes_two[m]) for m in range(8)]
    g_radius = jnp.sum(g_basis * d_basis, axis=0, keepdims=True) + spread(g_radius_pair)
    gux = r3 * g[1] + r15 * (g[4] * uy + g[7] * uz + g[8] * ux) - r5 * ux * g[6]
    guy = r3 * g[2] + r15 * (g[4] * ux + g[5] * uz - g[8] * uy) - r5 * uy * g[6]
    guz = r3 * g[3] + r15 * (g[5] * uy + g[7] * ux) + 2.0 * r5 * uz * g[6]
    radial_part = g_radius - inverse * (gux * ux + guy * uy + guz * uz)
    gd = [inverse * gu + u * radial_part for gu, u in ((gux, ux), (guy, uy), (guz, uz))]
    gd = jnp.concatenate(gd + [jnp.zeros((5, gd[0].shape[1]), F32)], axis=0)
    gr = slot(gd, 0)
    for k in range(1, slots):
        gr = gr + slot(gd, k)
    to_senders = jnp.concatenate([jnp.where(domain_s == float(d), gd, 0.0) for d in range(10)], axis=0)
    to_receivers = jnp.concatenate([jnp.where(domain_r == float(d), gr, 0.0) for d in range(10)], axis=0)
    to_all = jnp.concatenate(
        split(jnp.concatenate([to_senders, -to_receivers], axis=1)), axis=0
    )
    summed = dot(to_all, jnp.concatenate([hot_s, hot_r], axis=1), NT)
    grads[...] = (summed[: 9 * 8] + summed[10 * 8 : 19 * 8]).reshape(9, 8, atoms)
    copies = []
    for d in others:
        copy = pltpu.make_async_remote_copy(
            src_ref=grads.at[d],
            dst_ref=back.at[8 - d],
            send_sem=send_b.at[d],
            recv_sem=recv_b.at[8 - d],
            device_id=neighbour(d),
            device_id_type=pl.DeviceIdType.MESH,
        )
        copy.start()
        copies.append(copy)
    grads[4, 3:4, :] = energy
    copy = pltpu.make_async_copy(grads.at[4], back.at[4], send_b.at[4])
    copy.start()
    for copy in copies + [copy]:
        copy.wait()


def settle(back_ref, force_ref, energy_ref):
    total = back_ref[0]
    for d in range(1, 9):
        total = total + back_ref[d]
    for k in range(3):
        force_ref[0, k] = -total[k : k + 1]
    energy_ref[0] = back_ref[4, 3:4, :]


def local(positions, species, senders, counts, owners, send_list, embedding,
          radial_in_one, radial_mid_one, radial_out_one, mixing, square_mix, readout_one,
          radial_in_two, radial_mid_two, radial_out_two, mix_two, read_hidden, read_out):
    atoms = positions.shape[3]
    layers = atoms // (SIDE * SIDE)
    operands = (
        positions.transpose(0, 2, 1, 3), species, senders.transpose(0, 2, 1, 3), counts, send_list,
        owners.transpose(0, 2, 1, 3), embedding.T,
        radial_in_one.T, radial_mid_one, radial_out_one.T, mixing, square_mix, readout_one[None],
        radial_in_two.T, radial_mid_two, radial_out_two.T, mix_two, read_hidden, read_out[None],
    )
    vmem = pl.BlockSpec(memory_space=pltpu.VMEM)
    hbm = pl.BlockSpec(memory_space=pltpu.HBM)
    back = pl.pallas_call(
        functools.partial(kernel, layers),
        out_shape=jax.ShapeDtypeStruct((9, 8, atoms), F32),
        in_specs=[hbm] * len(operands),
        out_specs=hbm,
        scratch_shapes=[pltpu.VMEM(x.shape, x.dtype) for x in operands]
        + [
            pltpu.VMEM((9, ROWS, atoms), F32),
            pltpu.VMEM((9, 8, atoms), F32),
            pltpu.SemaphoreType.DMA((len(operands),)),
            pltpu.SemaphoreType.DMA((9,)),
            pltpu.SemaphoreType.DMA((9,)),
            pltpu.SemaphoreType.DMA((9,)),
            pltpu.SemaphoreType.DMA((9,)),
        ],
        compiler_params=pltpu.CompilerParams(
            collective_id=0, has_side_effects=True, vmem_limit_bytes=64 * 1024 * 1024
        ),
    )(*operands)
    forces, energies = pl.pallas_call(
        settle,
        out_shape=(
            jax.ShapeDtypeStruct(operands[0].shape, F32),
            jax.ShapeDtypeStruct(counts.shape, F32),
        ),
        in_specs=[vmem],
        out_specs=(vmem, vmem),
        compiler_params=pltpu.CompilerParams(vmem_limit_bytes=64 * 1024 * 1024),
    )(back)
    return forces.transpose(0, 2, 1, 3), energies


def solution(mesh):
    per_domain = (
        P("gx", "gy", None, None),
        P("gx", "gy", None),
        P("gx", "gy", None, None),
        P("gx", "gy", None),
        P("gx", "gy", None, None),
        P("gx", "gy", None),
    )
    return jax.shard_map(
        local,
        mesh=mesh,
        in_specs=per_domain + (P(),) * 13,
        out_specs=(P("gx", "gy", None, None), P("gx", "gy", None)),
        check_vma=False,
    )
```

```python
import functools
import math

import jax
import jax.numpy as jnp
from jax import lax
from jax.experimental import pallas as pl
from jax.experimental.pallas import tpu as pltpu
from jax.sharding import PartitionSpec as P

SIDE = 8
SPACING = 1.75
CUTOFF = 5.0
SOFTEN = 0.25
PAIR = 2.0
ROWS = 16
DEGREE = (0, 1, 1, 1, 2, 2, 2, 2, 2)
MEMBERS = ((0,), (1, 2, 3), (4, 5, 6, 7, 8))
F32 = jnp.float32
BF16 = jnp.bfloat16
NN = (((1,), (0,)), ((), ()))
NT = (((1,), (1,)), ((), ()))


def dot(a, b, dims=NN):
    return lax.dot_general(a, b, dims, preferred_element_type=F32)


def split(x):
    high = x.astype(BF16)
    return high, (x - high.astype(F32)).astype(BF16)


def split_three(x):
    high = x.astype(BF16)
    rest = x - high.astype(F32)
    return (high,) + split(rest)


def stack_left(x):
    high, low = split(x)
    high, low = high.astype(F32), low.astype(F32)
    return jnp.concatenate([high, low, high], axis=0).T.astype(BF16)


def left(x):
    high, low = split(x)
    lower = jnp.concatenate([low, jnp.zeros_like(low)], axis=1)
    return jnp.concatenate([jnp.concatenate([high, high], axis=1), lower], axis=0)


def mm_rows(left, b):
    out = dot(left, jnp.concatenate(split(b), axis=0))
    half = left.shape[0] // 2
    return out[:half] + out[half:]


def mm(left, b):
    high = b.astype(BF16).astype(F32)
    low = b - high
    if b.shape[0] % 16:
        right = jnp.concatenate([high, high, low], axis=0).astype(BF16)
    else:
        high, low = high.astype(BF16), low.astype(BF16)
        right = jnp.concatenate([high, high, low], axis=0)
    return dot(left, right)


def pick(parts, one_hot):
    return dot(jnp.concatenate(parts, axis=1), jnp.concatenate([one_hot] * len(parts), axis=0))


def put(parts, one_hot):
    return dot(jnp.concatenate(parts, axis=1), jnp.concatenate([one_hot] * len(parts), axis=1), NT)


def sin_cos_pi(t):
    turn = jnp.floor(t + 0.5)
    r = (t - turn) * math.pi
    sign = 1.0 - 2.0 * (turn - 2.0 * jnp.floor(turn * 0.5))
    z = r * r
    sine = jnp.full_like(z, 1.0 / math.factorial(13))
    cosine = jnp.full_like(z, -1.0 / math.factorial(14))
    for n in range(5, -1, -1):
        sine = sine * z + (-1.0) ** n / math.factorial(2 * n + 1)
    for n in range(6, -1, -1):
        cosine = cosine * z + (-1.0) ** n / math.factorial(2 * n)
    return sign * r * sine, sign * cosine


def floor_div(x, by):
    return jnp.floor((x + 0.5) * (1.0 / by))


def one_hot_rows(index, rows):
    ids = lax.broadcasted_iota(jnp.int32, (rows, index.shape[1]), 0).astype(F32)
    return jnp.where(ids == index, 1.0, 0.0).astype(BF16)


def by_domain(stacked, domain, rows):
    out = jnp.where(domain == 0.0, stacked[:rows], 0.0)
    for d in range(1, 9):
        out = out + jnp.where(domain == float(d), stacked[d * rows : (d + 1) * rows], 0.0)
    return out


def silu_pair(h):
    gate = 0.5 + 0.5 * jnp.tanh(0.5 * h)
    return h * gate, gate * (1.0 + h * (1.0 - gate))


def radial(nets):
    first = [silu_pair(mm(w_in, basis)) for basis, w_in, _, _ in nets]
    second = [silu_pair(mm(net[2], s[0])) for net, s in zip(nets, first)]
    return [(mm(net[3], s[0]), f[1], s[1]) for net, f, s in zip(nets, first, second)]


def radial_back(nets):
    upper = [mm_rows(net[3], net[0]) * net[5] for net in nets]
    lower = [mm(net[2], g) * net[4] for net, g in zip(nets, upper)]
    return [mm(net[1], g) for net, g in zip(nets, lower)]


def kernel(
    layers,
    *refs,
):
    inputs, back, held = refs[:19], refs[19], refs[20:39]
    table, grads, load, send_a, recv_a, send_b, recv_b = refs[39:]
    (
        pos_ref, spec_ref, send_ref, cnt_ref, list_ref, own_ref, emb_ref,
        wi1_ref, wm1_ref, wo1_ref, mix_ref, sqm_ref, ro1_ref,
        wi2_ref, wm2_ref, wo2_ref, mx2_ref, rh_ref, ro2_ref,
    ) = held
    atoms = pos_ref.shape[3]
    bound = list_ref.shape[2]
    slots = send_ref.shape[1]
    species, channels = emb_ref.shape
    nbasis = wi1_ref.shape[0]
    column = SIDE * layers
    wide = 2 * atoms
    ring = (SIDE + 2) * layers
    used = (SIDE + 2) * ring
    me_x, me_y = lax.axis_index("gx"), lax.axis_index("gy")
    nx, ny = lax.axis_size("gx"), lax.axis_size("gy")

    def neighbour(d):
        return (lax.rem(me_x + (d // 3 - 1) + nx, nx), lax.rem(me_y + (d % 3 - 1) + ny, ny))

    others = [d for d in range(9) if d != 4]
    barrier = pltpu.get_barrier_semaphore()
    for d in others:
        pl.semaphore_signal(barrier, inc=1, device_id=neighbour(d), device_id_type=pl.DeviceIdType.MESH)

    loads = [pltpu.make_async_copy(inputs[i], held[i], load.at[i]) for i in range(19)]
    for copy in loads:
        copy.start()
    table[4] = jnp.zeros((ROWS, atoms), F32)
    for copy in loads[:5]:
        copy.wait()
    for k in range(3):
        table[4, k : k + 1, :] = pos_ref[0, k]
    table[4, 3:4, :] = spec_ref[0].astype(F32)
    for k in range(slots):
        table[4, 4 + k : 5 + k, :] = send_ref[0, k].astype(F32)
    table[4, 7:8, :] = cnt_ref[0].astype(F32)
    table[4, 8:9, 0:bound] = list_ref[0].astype(F32)
    pl.semaphore_wait(barrier, 8)
    copies = []
    for d in others:
        copy = pltpu.make_async_remote_copy(
            src_ref=table.at[4],
            dst_ref=table.at[8 - d],
            send_sem=send_a.at[d],
            recv_sem=recv_a.at[8 - d],
            device_id=neighbour(d),
            device_id_type=pl.DeviceIdType.MESH,
        )
        copy.start()
        copies.append(copy)

    lane = lax.broadcasted_iota(jnp.int32, (1, wide), 1).astype(F32)
    ring_at = lane - atoms
    low_x = ring_at < ring
    long_side = ring_at < 2 * ring
    along = jnp.where(low_x, ring_at, ring_at - ring)
    in_y = ring_at - 2 * ring
    low_y = in_y < column
    across = jnp.where(low_y, in_y, in_y - column)
    half_long = floor_div(along, layers)
    half_short = floor_div(across, layers)
    site_x = jnp.where(long_side, jnp.where(low_x, -1.0, float(SIDE)), half_short)
    site_y = jnp.where(long_side, half_long - 1.0, jnp.where(low_y, -1.0, float(SIDE)))
    site_z = jnp.where(long_side, along - half_long * layers, across - half_short * layers)
    inside = (lane < atoms) | (lane >= used)
    off_x = jnp.where(inside, 0.0, floor_div(site_x, SIDE))
    off_y = jnp.where(inside, 0.0, floor_div(site_y, SIDE))
    ring_atom = (site_x - off_x * SIDE) * column + (site_y - off_y * SIDE) * layers + site_z
    atom_r = jnp.where(lane < atoms, lane, jnp.where(lane >= used, 0.0, ring_atom))
    domain_r = 3.0 * (off_x + 1.0) + (off_y + 1.0)
    hot_r = one_hot_rows(atom_r, atoms)

    for copy in loads[5:]:
        copy.wait()
    wi1, wi1_back = stack_left(wi1_ref[...]), stack_left(wi1_ref[...].T)
    wi2, wi2_back = stack_left(wi2_ref[...]), stack_left(wi2_ref[...].T)
    wm1, wm1_back = stack_left(wm1_ref[...].T), stack_left(wm1_ref[...])
    wm2, wm2_back = stack_left(wm2_ref[...].T), stack_left(wm2_ref[...])
    wo1, wo1_back = stack_left(wo1_ref[...]), left(wo1_ref[...])
    wo2, wo2_back = stack_left(wo2_ref[...]), left(wo2_ref[...])
    mix = [left(mix_ref[l]) for l in range(3)]
    mix_back = [left(mix_ref[l].T) for l in range(3)]
    sqm, sqm_back = left(sqm_ref[...]), left(sqm_ref[...].T)
    rh, rh_back = left(rh_ref[...]), stack_left(rh_ref[...])
    joined = mm_rows(rh, mx2_ref[...])
    both, both_back = left(joined), stack_left(joined)
    emb = split_three(emb_ref[...].T)
    ro1_cols = jnp.broadcast_to(ro1_ref[...], (atoms, channels)).T
    ro2_cols = jnp.broadcast_to(ro2_ref[...], (atoms, ro2_ref.shape[1])).T

    for copy in copies:
        copy.wait_recv()
    sent_first = copies

    def tile(x):
        return jnp.concatenate([x] * slots, axis=1)

    def slot(x, k):
        return x[:, k * wide : (k + 1) * wide]

    def own(x):
        return jnp.concatenate([x[:, k * wide : k * wide + atoms] for k in range(slots)], axis=1)

    def own_slot(x, k):
        return x[:, k * atoms : (k + 1) * atoms]

    def spread(x):
        zero = jnp.zeros((x.shape[0], atoms), F32)
        return jnp.concatenate([p for k in range(slots) for p in (own_slot(x, k), zero)], axis=1)

    everything = table[...].reshape(9 * ROWS, atoms)
    parts = split_three(everything)
    rec = by_domain(pick(parts, hot_r), domain_r, ROWS)
    sender = jnp.concatenate([rec[4 + k : 5 + k] for k in range(slots)], axis=1)
    live = jnp.concatenate(
        [jnp.where((rec[7:8] > float(k)) & (lane < used), 1.0, 0.0) for k in range(slots)], axis=1
    )
    is_local = sender < atoms
    ghost = sender - atoms
    block = floor_div(ghost, bound)
    place = ghost - block * bound
    block = jnp.where(block >= 4.0, block + 1.0, block)
    block = jnp.where(is_local, 4.0, block)
    block_x = floor_div(block, 3)
    block_y = block - 3.0 * block_x - 1.0
    block_x = block_x - 1.0
    to_x = tile(off_x) + block_x
    to_y = tile(off_y) + block_y
    domain_s = 3.0 * (to_x + 1.0) + (to_y + 1.0)
    lists = dot(parts[0], one_hot_rows(place, atoms))
    listed = jnp.zeros_like(sender)
    for d in range(9):
        listed = listed + jnp.where(domain_s == float(d), lists[d * ROWS + 8 : d * ROWS + 9], 0.0)
    atom_s = jnp.where(is_local, sender, listed)
    hot_s = one_hot_rows(atom_s, atoms)
    upper = jnp.concatenate([table[d, 0:8, :] for d in range(9)], axis=0)
    snd = by_domain(pick(split_three(upper), hot_s), domain_s, 8)

    side_length = SPACING * SIDE
    dx = (snd[0:1] + block_x * side_length) - tile(rec[0:1])
    dy = (snd[1:2] + block_y * side_length) - tile(rec[1:2])
    dz = snd[2:3] - tile(rec[2:3])
    radius = jnp.sqrt(dx * dx + dy * dy + dz * dz + SOFTEN)
    inverse = 1.0 / radius
    ux, uy, uz = dx * inverse, dy * inverse, dz * inverse
    x = jnp.minimum(radius / CUTOFF, 1.0)
    x2 = x * x
    x5 = x2 * x2 * x
    x6 = x5 * x
    envelope = 1.0 + x6 * (-28.0 + x * (48.0 - 21.0 * x))
    slope = jnp.where(radius < CUTOFF, 1.0 / CUTOFF, 0.0)
    d_envelope = x5 * (-168.0 + x * (336.0 - 168.0 * x)) * slope
    orders = (lax.broadcasted_iota(jnp.int32, (nbasis, 1), 0) + 1).astype(F32)
    scale = math.sqrt(2.0 / CUTOFF)
    sines, cosines = sin_cos_pi(orders * x)
    sines = sines * scale
    cosines = cosines * (orders * (scale * math.pi))
    basis = sines * (inverse * envelope)
    d_basis = cosines * (slope * inverse * envelope) + sines * (
        inverse * d_envelope - inverse * inverse * envelope
    )
    r3, r5, r15 = math.sqrt(3.0), math.sqrt(5.0), math.sqrt(15.0)
    shapes = [
        None,
        r3 * ux,
        r3 * uy,
        r3 * uz,
        r15 * ux * uy,
        r15 * uy * uz,
        0.5 * r5 * (2.0 * uz * uz - ux * ux - uy * uy),
        r15 * ux * uz,
        0.5 * r15 * (ux * ux - uy * uy),
    ]

    def rows_of(w, l):
        return w[l * channels : (l + 1) * channels]

    species_row = lax.broadcasted_iota(jnp.int32, (species, 1), 0).astype(F32)
    hot_es = jnp.where(species_row == snd[3:4], 1.0, 0.0).astype(BF16)
    hot_er = jnp.where(species_row == rec[3:4], 1.0, 0.0).astype(BF16)
    carrier = pick(emb, hot_es) * (live * (1.0 / slots))
    embedded = pick(emb, hot_er)
    (edge_one, one_g1, one_g2), (edge_two, two_g1, two_g2) = radial(
        [(basis, wi1, wm1, wo1), (own(basis), wi2, wm2, wo2)]
    )
    carried = [rows_of(edge_one, l) * carrier for l in range(3)]
    moments = []
    for m in range(9):
        term = carried[DEGREE[m]] if m == 0 else carried[DEGREE[m]] * shapes[m]
        total = slot(term, 0)
        for k in range(1, slots):
            total = total + slot(term, k)
        moments.append(total)
    squares = moments[0] * moments[0]
    for m in range(1, 9):
        squares = squares + moments[m] * moments[m]
    features = [mm_rows(mix[0], moments[0]) + mm_rows(sqm, squares) + embedded]
    for l in (1, 2):
        mixed = mm_rows(mix[l], jnp.concatenate([moments[m] for m in MEMBERS[l]], axis=1))
        features += [mixed[:, i * wide : (i + 1) * wide] for i in range(len(MEMBERS[l]))]

    live_two = own(live) * (1.0 / slots)
    shapes_two = [None] + [own(s) for s in shapes[1:]]
    at_two, to_x2, to_y2 = own(atom_s), own(to_x), own(to_y)
    ax = floor_div(at_two, column)
    rest = at_two - ax * column
    ay = floor_div(rest, layers)
    az = rest - ay * layers
    sx = ax + to_x2 * SIDE
    sy = ay + to_y2 * SIDE
    outside = jnp.where(
        to_x2 != 0.0,
        jnp.where(to_x2 < 0.0, 0.0, float(ring)) + (sy + 1.0) * layers + az,
        2.0 * ring + jnp.where(to_y2 < 0.0, 0.0, float(column)) + sx * layers + az,
    )
    at_ring = jnp.where((to_x2 == 0.0) & (to_y2 == 0.0), at_two, atoms + outside)
    hot_two = one_hot_rows(at_ring, wide)
    stacked = jnp.concatenate(features, axis=0)
    sent = pick(split(stacked), hot_two)
    projected = []
    for l in range(3):
        total = None
        for m in MEMBERS[l]:
            term = rows_of(sent, m) if m == 0 else rows_of(sent, m) * shapes_two[m]
            total = term if total is None else total + term
        projected.append(total)
    scalar = sum(rows_of(edge_two, l) * projected[l] for l in range(3)) * live_two
    gathered = own_slot(scalar, 0)
    for k in range(1, slots):
        gathered = gathered + own_slot(scalar, k)
    hidden, hidden_slope = silu_pair(mm_rows(both, gathered) + mm_rows(rh, features[0][:, :atoms]))
    owners = jnp.concatenate([own_ref[0, k].astype(F32) for k in range(slots)], axis=1)
    decay = PAIR * jnp.exp(-own(radius)) * owners * own(live)
    g_radius_pair = decay * (own(d_envelope) - own(envelope))

    g_hidden = ro2_cols * hidden_slope
    g_refined = mm(rh_back, g_hidden)
    g_gathered = mm(both_back, g_hidden)
    t = jnp.concatenate([g_gathered] * slots, axis=1) * live_two
    g_edge_two = jnp.concatenate([t * projected[l] for l in range(3)], axis=0)
    g_proj = [t * rows_of(edge_two, l) for l in range(3)]
    g_sent = jnp.concatenate(
        [g_proj[0]] + [g_proj[DEGREE[m]] * shapes_two[m] for m in range(1, 9)], axis=0
    )
    g_shapes_two = [
        jnp.sum(g_proj[DEGREE[m]] * rows_of(sent, m), axis=0, keepdims=True) for m in range(1, 9)
    ]
    g_stacked = put(split(g_sent), hot_two)
    g_features = [rows_of(g_stacked, m) for m in range(9)]
    g_features[0] = g_features[0] + jnp.concatenate(
        [g_refined + ro1_cols, jnp.zeros((channels, wide - atoms), F32)], axis=1
    )

    g_squares = mm_rows(sqm_back, g_features[0]) * 2.0
    g_moments = [mm_rows(mix_back[0], g_features[0])]
    for l in (1, 2):
        mixed = mm_rows(mix_back[l], jnp.concatenate([g_features[m] for m in MEMBERS[l]], axis=1))
        g_moments += [mixed[:, i * wide : (i + 1) * wide] for i in range(len(MEMBERS[l]))]
    g_moments = [g + g_squares * moments[m] for m, g in enumerate(g_moments)]
    g_edge_one = []
    g_shapes = []
    for l in range(3):
        total = None
        for m in MEMBERS[l]:
            tiled = tile(g_moments[m])
            term = tiled if m == 0 else tiled * shapes[m]
            total = term if total is None else total + term
            if m > 0:
                g_shapes.append(jnp.sum(tiled * carried[l], axis=0, keepdims=True))
        g_edge_one.append(total * carrier)
    g_basis, g_basis_two = radial_back(
        [
            (jnp.concatenate(g_edge_one, axis=0), wi1_back, wm1_back, wo1_back, one_g1, one_g2),
            (g_edge_two, wi2_back, wm2_back, wo2_back, two_g1, two_g2),
        ]
    )

    g_basis = g_basis + spread(g_basis_two)
    g = [None] + [g_shapes[m] + spread(g_shapes_two[m]) for m in range(8)]
    g_radius = jnp.sum(g_basis * d_basis, axis=0, keepdims=True) + spread(g_radius_pair)
    gux = r3 * g[1] + r15 * (g[4] * uy + g[7] * uz + g[8] * ux) - r5 * ux * g[6]
    guy = r3 * g[2] + r15 * (g[4] * ux + g[5] * uz - g[8] * uy) - r5 * uy * g[6]
    guz = r3 * g[3] + r15 * (g[5] * uy + g[7] * ux) + 2.0 * r5 * uz * g[6]
    radial_part = g_radius - inverse * (gux * ux + guy * uy + guz * uz)
    gd = [inverse * gu + u * radial_part for gu, u in ((gux, ux), (guy, uy), (guz, uz))]
    gd = jnp.concatenate(gd + [jnp.zeros((5, gd[0].shape[1]), F32)], axis=0)
    gr = slot(gd, 0)
    for k in range(1, slots):
        gr = gr + slot(gd, k)
    to_senders = jnp.concatenate([jnp.where(domain_s == float(d), gd, 0.0) for d in range(10)], axis=0)
    to_receivers = jnp.concatenate([jnp.where(domain_r == float(d), gr, 0.0) for d in range(10)], axis=0)
    to_all = jnp.concatenate(
        split(jnp.concatenate([to_senders, -to_receivers], axis=1)), axis=0
    )
    summed = dot(to_all, jnp.concatenate([hot_s, hot_r], axis=1), NT)
    grads[...] = (summed[: 9 * 8] + summed[10 * 8 : 19 * 8]).reshape(9, 8, atoms)
    copies = []
    for d in others:
        copy = pltpu.make_async_remote_copy(
            src_ref=grads.at[d],
            dst_ref=back.at[8 - d],
            send_sem=send_b.at[d],
            recv_sem=recv_b.at[8 - d],
            device_id=neighbour(d),
            device_id_type=pl.DeviceIdType.MESH,
        )
        copy.start()
        copies.append(copy)
    energy_two = jnp.sum(ro2_cols * hidden, axis=0, keepdims=True)
    energy_one = jnp.sum(ro1_cols * features[0][:, :atoms], axis=0, keepdims=True)
    pair = decay * own(envelope)
    energy = energy_one + energy_two
    for k in range(slots):
        energy = energy + own_slot(pair, k)
    grads[4, 3:4, :] = energy
    copy = pltpu.make_async_copy(grads.at[4], back.at[4], send_b.at[4])
    copy.start()
    for copy in copies + [copy]:
        copy.wait()
    for copy in sent_first:
        copy.wait_send()


def settle(back_ref, force_ref, energy_ref):
    total = back_ref[0]
    for d in range(1, 9):
        total = total + back_ref[d]
    for k in range(3):
        force_ref[0, k] = -total[k : k + 1]
    energy_ref[0] = back_ref[4, 3:4, :]


def local(positions, species, senders, counts, owners, send_list, embedding,
          radial_in_one, radial_mid_one, radial_out_one, mixing, square_mix, readout_one,
          radial_in_two, radial_mid_two, radial_out_two, mix_two, read_hidden, read_out):
    atoms = positions.shape[3]
    layers = atoms // (SIDE * SIDE)
    operands = (
        positions.transpose(0, 2, 1, 3), species, senders.transpose(0, 2, 1, 3), counts, send_list,
        owners.transpose(0, 2, 1, 3), embedding.T,
        radial_in_one.T, radial_mid_one, radial_out_one.T, mixing, square_mix, readout_one[None],
        radial_in_two.T, radial_mid_two, radial_out_two.T, mix_two, read_hidden, read_out[None],
    )
    vmem = pl.BlockSpec(memory_space=pltpu.VMEM)
    hbm = pl.BlockSpec(memory_space=pltpu.HBM)
    back = pl.pallas_call(
        functools.partial(kernel, layers),
        out_shape=jax.ShapeDtypeStruct((9, 8, atoms), F32),
        in_specs=[hbm] * len(operands),
        out_specs=hbm,
        scratch_shapes=[pltpu.VMEM(x.shape, x.dtype) for x in operands]
        + [
            pltpu.VMEM((9, ROWS, atoms), F32),
            pltpu.VMEM((9, 8, atoms), F32),
            pltpu.SemaphoreType.DMA((len(operands),)),
            pltpu.SemaphoreType.DMA((9,)),
            pltpu.SemaphoreType.DMA((9,)),
            pltpu.SemaphoreType.DMA((9,)),
            pltpu.SemaphoreType.DMA((9,)),
        ],
        compiler_params=pltpu.CompilerParams(
            collective_id=0, has_side_effects=True, vmem_limit_bytes=64 * 1024 * 1024
        ),
    )(*operands)
    forces, energies = pl.pallas_call(
        settle,
        out_shape=(
            jax.ShapeDtypeStruct(operands[0].shape, F32),
            jax.ShapeDtypeStruct(counts.shape, F32),
        ),
        in_specs=[vmem],
        out_specs=(vmem, vmem),
        compiler_params=pltpu.CompilerParams(vmem_limit_bytes=64 * 1024 * 1024),
    )(back)
    return forces.transpose(0, 2, 1, 3), energies


def solution(mesh):
    per_domain = (
        P("gx", "gy", None, None),
        P("gx", "gy", None),
        P("gx", "gy", None, None),
        P("gx", "gy", None),
        P("gx", "gy", None, None),
        P("gx", "gy", None),
    )
    return jax.shard_map(
        local,
        mesh=mesh,
        in_specs=per_domain + (P(),) * 13,
        out_specs=(P("gx", "gy", None, None), P("gx", "gy", None)),
        check_vma=False,
    )
```

```python
import functools
import math

import jax
import jax.numpy as jnp
from jax import lax
from jax.experimental import pallas as pl
from jax.experimental.pallas import tpu as pltpu
from jax.sharding import PartitionSpec as P

SIDE = 8
SPACING = 1.75
CUTOFF = 5.0
SOFTEN = 0.25
PAIR = 2.0
ROWS = 16
DEGREE = (0, 1, 1, 1, 2, 2, 2, 2, 2)
MEMBERS = ((0,), (1, 2, 3), (4, 5, 6, 7, 8))
F32 = jnp.float32
BF16 = jnp.bfloat16
NN = (((1,), (0,)), ((), ()))
NT = (((1,), (1,)), ((), ()))


def dot(a, b, dims=NN):
    return lax.dot_general(a, b, dims, preferred_element_type=F32)


def split(x):
    high = x.astype(BF16)
    return high, (x - high.astype(F32)).astype(BF16)


def split_three(x):
    high = x.astype(BF16)
    rest = x - high.astype(F32)
    return (high,) + split(rest)


def stack_left(x):
    high, low = split(x)
    high, low = high.astype(F32), low.astype(F32)
    return jnp.concatenate([high, low, high], axis=0).T.astype(BF16)


def left(x):
    high, low = split(x)
    lower = jnp.concatenate([low, jnp.zeros_like(low)], axis=1)
    return jnp.concatenate([jnp.concatenate([high, high], axis=1), lower], axis=0)


def mm_rows(left, b):
    out = dot(left, jnp.concatenate(split(b), axis=0))
    half = left.shape[0] // 2
    return out[:half] + out[half:]


def mm(left, b):
    high = b.astype(BF16).astype(F32)
    low = b - high
    if b.shape[0] % 16:
        right = jnp.concatenate([high, high, low], axis=0).astype(BF16)
    else:
        high, low = high.astype(BF16), low.astype(BF16)
        right = jnp.concatenate([high, high, low], axis=0)
    return dot(left, right)


def pick(parts, one_hot):
    return dot(jnp.concatenate(parts, axis=1), jnp.concatenate([one_hot] * len(parts), axis=0))


def put(parts, one_hot):
    return dot(jnp.concatenate(parts, axis=1), jnp.concatenate([one_hot] * len(parts), axis=1), NT)


def sin_cos_pi(t):
    turn = jnp.floor(t + 0.5)
    r = (t - turn) * math.pi
    sign = 1.0 - 2.0 * (turn - 2.0 * jnp.floor(turn * 0.5))
    z = r * r
    sine = jnp.full_like(z, 1.0 / math.factorial(13))
    cosine = jnp.full_like(z, -1.0 / math.factorial(14))
    for n in range(5, -1, -1):
        sine = sine * z + (-1.0) ** n / math.factorial(2 * n + 1)
    for n in range(6, -1, -1):
        cosine = cosine * z + (-1.0) ** n / math.factorial(2 * n)
    return sign * r * sine, sign * cosine


def floor_div(x, by):
    return jnp.floor((x + 0.5) * (1.0 / by))


def one_hot_rows(index, rows):
    ids = lax.broadcasted_iota(jnp.int32, (rows, index.shape[1]), 0).astype(F32)
    return jnp.where(ids == index, 1.0, 0.0).astype(BF16)


def by_domain(stacked, domain, rows):
    out = jnp.where(domain == 0.0, stacked[:rows], 0.0)
    for d in range(1, 9):
        out = out + jnp.where(domain == float(d), stacked[d * rows : (d + 1) * rows], 0.0)
    return out


def silu_pair(h):
    gate = 0.5 + 0.5 * jnp.tanh(0.5 * h)
    return h * gate, gate * (1.0 + h * (1.0 - gate))


def radial(nets):
    first = [silu_pair(mm(w_in, basis)) for basis, w_in, _, _ in nets]
    second = [silu_pair(mm(net[2], s[0])) for net, s in zip(nets, first)]
    return [(mm(net[3], s[0]), f[1], s[1]) for net, f, s in zip(nets, first, second)]


def radial_back(nets):
    upper = [mm_rows(net[3], net[0]) * net[5] for net in nets]
    lower = [mm(net[2], g) * net[4] for net, g in zip(nets, upper)]
    return [mm(net[1], g) for net, g in zip(nets, lower)]


def kernel(
    layers,
    *refs,
):
    inputs, back, held = refs[:19], refs[19], refs[20:39]
    table, grads, load, send_a, recv_a, send_b, recv_b = refs[39:]
    (
        pos_ref, spec_ref, send_ref, cnt_ref, list_ref, own_ref, emb_ref,
        wi1_ref, wm1_ref, wo1_ref, mix_ref, sqm_ref, ro1_ref,
        wi2_ref, wm2_ref, wo2_ref, mx2_ref, rh_ref, ro2_ref,
    ) = held
    atoms = pos_ref.shape[3]
    bound = list_ref.shape[2]
    slots = send_ref.shape[1]
    species, channels = emb_ref.shape
    nbasis = wi1_ref.shape[0]
    column = SIDE * layers
    wide = 2 * atoms
    ring = (SIDE + 2) * layers
    used = (SIDE + 2) * ring
    me_x, me_y = lax.axis_index("gx"), lax.axis_index("gy")
    nx, ny = lax.axis_size("gx"), lax.axis_size("gy")

    def neighbour(d):
        return (lax.rem(me_x + (d // 3 - 1) + nx, nx), lax.rem(me_y + (d % 3 - 1) + ny, ny))

    others = [d for d in range(9) if d != 4]
    barrier = pltpu.get_barrier_semaphore()
    for d in others:
        pl.semaphore_signal(barrier, inc=1, device_id=neighbour(d), device_id_type=pl.DeviceIdType.MESH)

    loads = [pltpu.make_async_copy(inputs[i], held[i], load.at[i]) for i in range(19)]
    for copy in loads:
        copy.start()
    table[4] = jnp.zeros((ROWS, atoms), F32)
    for copy in loads[:5]:
        copy.wait()
    for k in range(3):
        table[4, k : k + 1, :] = pos_ref[0, k]
    table[4, 3:4, :] = spec_ref[0].astype(F32)
    for k in range(slots):
        table[4, 4 + k : 5 + k, :] = send_ref[0, k].astype(F32)
    table[4, 7:8, :] = cnt_ref[0].astype(F32)
    table[4, 8:9, 0:bound] = list_ref[0].astype(F32)
    pl.semaphore_wait(barrier, 8)
    copies = []
    for d in others:
        copy = pltpu.make_async_remote_copy(
            src_ref=table.at[4],
            dst_ref=table.at[8 - d],
            send_sem=send_a.at[d],
            recv_sem=recv_a.at[8 - d],
            device_id=neighbour(d),
            device_id_type=pl.DeviceIdType.MESH,
        )
        copy.start()
        copies.append(copy)

    lane = lax.broadcasted_iota(jnp.int32, (1, wide), 1).astype(F32)
    ring_at = lane - atoms
    low_x = ring_at < ring
    long_side = ring_at < 2 * ring
    along = jnp.where(low_x, ring_at, ring_at - ring)
    in_y = ring_at - 2 * ring
    low_y = in_y < column
    across = jnp.where(low_y, in_y, in_y - column)
    half_long = floor_div(along, layers)
    half_short = floor_div(across, layers)
    site_x = jnp.where(long_side, jnp.where(low_x, -1.0, float(SIDE)), half_short)
    site_y = jnp.where(long_side, half_long - 1.0, jnp.where(low_y, -1.0, float(SIDE)))
    site_z = jnp.where(long_side, along - half_long * layers, across - half_short * layers)
    inside = (lane < atoms) | (lane >= used)
    off_x = jnp.where(inside, 0.0, floor_div(site_x, SIDE))
    off_y = jnp.where(inside, 0.0, floor_div(site_y, SIDE))
    ring_atom = (site_x - off_x * SIDE) * column + (site_y - off_y * SIDE) * layers + site_z
    atom_r = jnp.where(lane < atoms, lane, jnp.where(lane >= used, 0.0, ring_atom))
    domain_r = 3.0 * (off_x + 1.0) + (off_y + 1.0)
    hot_r = one_hot_rows(atom_r, atoms)

    for copy in loads[5:]:
        copy.wait()
    wi1, wi1_back = stack_left(wi1_ref[...]), stack_left(wi1_ref[...].T)
    wi2, wi2_back = stack_left(wi2_ref[...]), stack_left(wi2_ref[...].T)
    wm1, wm1_back = stack_left(wm1_ref[...].T), stack_left(wm1_ref[...])
    wm2, wm2_back = stack_left(wm2_ref[...].T), stack_left(wm2_ref[...])
    wo1, wo1_back = stack_left(wo1_ref[...]), left(wo1_ref[...])
    wo2, wo2_back = stack_left(wo2_ref[...]), left(wo2_ref[...])
    mix = [left(mix_ref[l]) for l in range(3)]
    mix_back = [left(mix_ref[l].T) for l in range(3)]
    sqm, sqm_back = left(sqm_ref[...]), left(sqm_ref[...].T)
    rh, rh_back = left(rh_ref[...]), stack_left(rh_ref[...])
    joined = mm_rows(rh, mx2_ref[...])
    both, both_back = left(joined), stack_left(joined)
    emb = split_three(emb_ref[...].T)
    ro1_cols = jnp.broadcast_to(ro1_ref[...], (atoms, channels)).T
    ro2_cols = jnp.broadcast_to(ro2_ref[...], (atoms, ro2_ref.shape[1])).T

    for copy in copies:
        copy.wait_recv()
    sent_first = copies

    def tile(x):
        return jnp.concatenate([x] * slots, axis=1)

    def slot(x, k):
        return x[:, k * wide : (k + 1) * wide]

    def own(x):
        return jnp.concatenate([x[:, k * wide : k * wide + atoms] for k in range(slots)], axis=1)

    def own_slot(x, k):
        return x[:, k * atoms : (k + 1) * atoms]

    def spread(x):
        zero = jnp.zeros((x.shape[0], atoms), F32)
        return jnp.concatenate([p for k in range(slots) for p in (own_slot(x, k), zero)], axis=1)

    everything = table[...].reshape(9 * ROWS, atoms)
    parts = split_three(everything)
    rec = by_domain(pick(parts, hot_r), domain_r, ROWS)
    sender = jnp.concatenate([rec[4 + k : 5 + k] for k in range(slots)], axis=1)
    live = jnp.concatenate(
        [jnp.where((rec[7:8] > float(k)) & (lane < used), 1.0, 0.0) for k in range(slots)], axis=1
    )
    is_local = sender < atoms
    ghost = sender - atoms
    block = floor_div(ghost, bound)
    place = ghost - block * bound
    block = jnp.where(block >= 4.0, block + 1.0, block)
    block = jnp.where(is_local, 4.0, block)
    block_x = floor_div(block, 3)
    block_y = block - 3.0 * block_x - 1.0
    block_x = block_x - 1.0
    to_x = tile(off_x) + block_x
    to_y = tile(off_y) + block_y
    domain_s = 3.0 * (to_x + 1.0) + (to_y + 1.0)
    lists = dot(parts[0], one_hot_rows(place, atoms))
    listed = jnp.zeros_like(sender)
    for d in range(9):
        listed = listed + jnp.where(domain_s == float(d), lists[d * ROWS + 8 : d * ROWS + 9], 0.0)
    atom_s = jnp.where(is_local, sender, listed)
    hot_s = one_hot_rows(atom_s, atoms)
    upper = jnp.concatenate([table[d, 0:8, :] for d in range(9)], axis=0)
    snd = by_domain(pick(split_three(upper), hot_s), domain_s, 8)

    side_length = SPACING * SIDE
    dx = (snd[0:1] + block_x * side_length) - tile(rec[0:1])
    dy = (snd[1:2] + block_y * side_length) - tile(rec[1:2])
    dz = snd[2:3] - tile(rec[2:3])
    radius = jnp.sqrt(dx * dx + dy * dy + dz * dz + SOFTEN)
    inverse = 1.0 / radius
    ux, uy, uz = dx * inverse, dy * inverse, dz * inverse
    x = jnp.minimum(radius / CUTOFF, 1.0)
    x2 = x * x
    x5 = x2 * x2 * x
    x6 = x5 * x
    envelope = 1.0 + x6 * (-28.0 + x * (48.0 - 21.0 * x))
    slope = jnp.where(radius < CUTOFF, 1.0 / CUTOFF, 0.0)
    d_envelope = x5 * (-168.0 + x * (336.0 - 168.0 * x)) * slope
    orders = (lax.broadcasted_iota(jnp.int32, (nbasis, 1), 0) + 1).astype(F32)
    scale = math.sqrt(2.0 / CUTOFF)
    sines, cosines = sin_cos_pi(orders * x)
    sines = sines * scale
    cosines = cosines * (orders * (scale * math.pi))
    basis = sines * (inverse * envelope)
    d_basis = cosines * (slope * inverse * envelope) + sines * (
        inverse * d_envelope - inverse * inverse * envelope
    )
    r3, r5, r15 = math.sqrt(3.0), math.sqrt(5.0), math.sqrt(15.0)
    shapes = [
        None,
        r3 * ux,
        r3 * uy,
        r3 * uz,
        r15 * ux * uy,
        r15 * uy * uz,
        0.5 * r5 * (2.0 * uz * uz - ux * ux - uy * uy),
        r15 * ux * uz,
        0.5 * r15 * (ux * ux - uy * uy),
    ]

    def rows_of(w, l):
        return w[l * channels : (l + 1) * channels]

    species_row = lax.broadcasted_iota(jnp.int32, (species, 1), 0).astype(F32)
    hot_es = jnp.where(species_row == snd[3:4], 1.0, 0.0).astype(BF16)
    hot_er = jnp.where(species_row == rec[3:4], 1.0, 0.0).astype(BF16)
    carrier = pick(emb, hot_es) * (live * (1.0 / slots))
    embedded = pick(emb, hot_er)
    (edge_one, one_g1, one_g2), (edge_two, two_g1, two_g2) = radial(
        [(basis, wi1, wm1, wo1), (own(basis), wi2, wm2, wo2)]
    )
    carried = [rows_of(edge_one, l) * carrier for l in range(3)]
    moments = []
    for m in range(9):
        term = carried[DEGREE[m]] if m == 0 else carried[DEGREE[m]] * shapes[m]
        total = slot(term, 0)
        for k in range(1, slots):
            total = total + slot(term, k)
        moments.append(total)
    squares = moments[0] * moments[0]
    for m in range(1, 9):
        squares = squares + moments[m] * moments[m]
    features = [mm_rows(mix[0], moments[0]) + mm_rows(sqm, squares) + embedded]
    for l in (1, 2):
        mixed = mm_rows(mix[l], jnp.concatenate([moments[m] for m in MEMBERS[l]], axis=1))
        features += [mixed[:, i * wide : (i + 1) * wide] for i in range(len(MEMBERS[l]))]

    live_two = own(live) * (1.0 / slots)
    shapes_two = [None] + [own(s) for s in shapes[1:]]
    at_two, to_x2, to_y2 = own(atom_s), own(to_x), own(to_y)
    ax = floor_div(at_two, column)
    rest = at_two - ax * column
    ay = floor_div(rest, layers)
    az = rest - ay * layers
    sx = ax + to_x2 * SIDE
    sy = ay + to_y2 * SIDE
    outside = jnp.where(
        to_x2 != 0.0,
        jnp.where(to_x2 < 0.0, 0.0, float(ring)) + (sy + 1.0) * layers + az,
        2.0 * ring + jnp.where(to_y2 < 0.0, 0.0, float(column)) + sx * layers + az,
    )
    at_ring = jnp.where((to_x2 == 0.0) & (to_y2 == 0.0), at_two, atoms + outside)
    hot_two = one_hot_rows(at_ring, wide)
    stacked = jnp.concatenate(features, axis=0)
    sent = pick(split(stacked), hot_two)
    projected = []
    for l in range(3):
        total = None
        for m in MEMBERS[l]:
            term = rows_of(sent, m) if m == 0 else rows_of(sent, m) * shapes_two[m]
            total = term if total is None else total + term
        projected.append(total)
    scalar = sum(rows_of(edge_two, l) * projected[l] for l in range(3)) * live_two
    gathered = own_slot(scalar, 0)
    for k in range(1, slots):
        gathered = gathered + own_slot(scalar, k)
    hidden, hidden_slope = silu_pair(mm_rows(both, gathered) + mm_rows(rh, features[0][:, :atoms]))
    owners = jnp.concatenate([own_ref[0, k].astype(F32) for k in range(slots)], axis=1)
    decay = PAIR * jnp.exp(-own(radius)) * owners * own(live)
    g_radius_pair = decay * (own(d_envelope) - own(envelope))

    g_hidden = ro2_cols * hidden_slope
    g_refined = mm(rh_back, g_hidden)
    g_gathered = mm(both_back, g_hidden)
    t = jnp.concatenate([g_gathered] * slots, axis=1) * live_two
    g_proj = [t * rows_of(edge_two, l) for l in range(3)]
    g_sent = jnp.concatenate(
        [g_proj[0]] + [g_proj[DEGREE[m]] * shapes_two[m] for m in range(1, 9)], axis=0
    )
    g_stacked = put(split(g_sent), hot_two)
    g_shapes_two = [
        jnp.sum(g_proj[DEGREE[m]] * rows_of(sent, m), axis=0, keepdims=True) for m in range(1, 9)
    ]
    g_edge_two = jnp.concatenate([t * projected[l] for l in range(3)], axis=0)
    g_features = [rows_of(g_stacked, m) for m in range(9)]
    g_features[0] = g_features[0] + jnp.concatenate(
        [g_refined + ro1_cols, jnp.zeros((channels, wide - atoms), F32)], axis=1
    )

    g_squares = mm_rows(sqm_back, g_features[0]) * 2.0
    g_moments = [mm_rows(mix_back[0], g_features[0])]
    for l in (1, 2):
        mixed = mm_rows(mix_back[l], jnp.concatenate([g_features[m] for m in MEMBERS[l]], axis=1))
        g_moments += [mixed[:, i * wide : (i + 1) * wide] for i in range(len(MEMBERS[l]))]
    g_moments = [g + g_squares * moments[m] for m, g in enumerate(g_moments)]
    g_edge_one = []
    g_shapes = []
    for l in range(3):
        total = None
        for m in MEMBERS[l]:
            tiled = tile(g_moments[m])
            term = tiled if m == 0 else tiled * shapes[m]
            total = term if total is None else total + term
            if m > 0:
                g_shapes.append(jnp.sum(tiled * carried[l], axis=0, keepdims=True))
        g_edge_one.append(total * carrier)
    g_basis, g_basis_two = radial_back(
        [
            (jnp.concatenate(g_edge_one, axis=0), wi1_back, wm1_back, wo1_back, one_g1, one_g2),
            (g_edge_two, wi2_back, wm2_back, wo2_back, two_g1, two_g2),
        ]
    )

    g_basis = g_basis + spread(g_basis_two)
    g = [None] + [g_shapes[m] + spread(g_shapes_two[m]) for m in range(8)]
    g_radius = jnp.sum(g_basis * d_basis, axis=0, keepdims=True) + spread(g_radius_pair)
    gux = r3 * g[1] + r15 * (g[4] * uy + g[7] * uz + g[8] * ux) - r5 * ux * g[6]
    guy = r3 * g[2] + r15 * (g[4] * ux + g[5] * uz - g[8] * uy) - r5 * uy * g[6]
    guz = r3 * g[3] + r15 * (g[5] * uy + g[7] * ux) + 2.0 * r5 * uz * g[6]
    radial_part = g_radius - inverse * (gux * ux + guy * uy + guz * uz)
    gd = [inverse * gu + u * radial_part for gu, u in ((gux, ux), (guy, uy), (guz, uz))]
    gd = jnp.concatenate(gd + [jnp.zeros((5, gd[0].shape[1]), F32)], axis=0)
    gr = slot(gd, 0)
    for k in range(1, slots):
        gr = gr + slot(gd, k)
    to_senders = jnp.concatenate([jnp.where(domain_s == float(d), gd, 0.0) for d in range(10)], axis=0)
    to_receivers = jnp.concatenate([jnp.where(domain_r == float(d), gr, 0.0) for d in range(10)], axis=0)
    to_all = jnp.concatenate(
        split(jnp.concatenate([to_senders, -to_receivers], axis=1)), axis=0
    )
    summed = dot(to_all, jnp.concatenate([hot_s, hot_r], axis=1), NT)
    grads[...] = (summed[: 9 * 8] + summed[10 * 8 : 19 * 8]).reshape(9, 8, atoms)
    copies = []
    for d in others:
        copy = pltpu.make_async_remote_copy(
            src_ref=grads.at[d],
            dst_ref=back.at[8 - d],
            send_sem=send_b.at[d],
            recv_sem=recv_b.at[8 - d],
            device_id=neighbour(d),
            device_id_type=pl.DeviceIdType.MESH,
        )
        copy.start()
        copies.append(copy)
    energy_two = jnp.sum(ro2_cols * hidden, axis=0, keepdims=True)
    energy_one = jnp.sum(ro1_cols * features[0][:, :atoms], axis=0, keepdims=True)
    pair = decay * own(envelope)
    energy = energy_one + energy_two
    for k in range(slots):
        energy = energy + own_slot(pair, k)
    grads[4, 3:4, :] = energy
    copy = pltpu.make_async_copy(grads.at[4], back.at[4], send_b.at[4])
    copy.start()
    for copy in copies + [copy]:
        copy.wait()
    for copy in sent_first:
        copy.wait_send()


def settle(back_ref, force_ref, energy_ref):
    total = back_ref[0]
    for d in range(1, 9):
        total = total + back_ref[d]
    for k in range(3):
        force_ref[0, k] = -total[k : k + 1]
    energy_ref[0] = back_ref[4, 3:4, :]


def local(positions, species, senders, counts, owners, send_list, embedding,
          radial_in_one, radial_mid_one, radial_out_one, mixing, square_mix, readout_one,
          radial_in_two, radial_mid_two, radial_out_two, mix_two, read_hidden, read_out):
    atoms = positions.shape[3]
    layers = atoms // (SIDE * SIDE)
    operands = (
        positions.transpose(0, 2, 1, 3), species, senders.transpose(0, 2, 1, 3), counts, send_list,
        owners.transpose(0, 2, 1, 3), embedding.T,
        radial_in_one.T, radial_mid_one, radial_out_one.T, mixing, square_mix, readout_one[None],
        radial_in_two.T, radial_mid_two, radial_out_two.T, mix_two, read_hidden, read_out[None],
    )
    vmem = pl.BlockSpec(memory_space=pltpu.VMEM)
    hbm = pl.BlockSpec(memory_space=pltpu.HBM)
    back = pl.pallas_call(
        functools.partial(kernel, layers),
        out_shape=jax.ShapeDtypeStruct((9, 8, atoms), F32),
        in_specs=[hbm] * len(operands),
        out_specs=hbm,
        scratch_shapes=[pltpu.VMEM(x.shape, x.dtype) for x in operands]
        + [
            pltpu.VMEM((9, ROWS, atoms), F32),
            pltpu.VMEM((9, 8, atoms), F32),
            pltpu.SemaphoreType.DMA((len(operands),)),
            pltpu.SemaphoreType.DMA((9,)),
            pltpu.SemaphoreType.DMA((9,)),
            pltpu.SemaphoreType.DMA((9,)),
            pltpu.SemaphoreType.DMA((9,)),
        ],
        compiler_params=pltpu.CompilerParams(
            collective_id=0, has_side_effects=True, vmem_limit_bytes=64 * 1024 * 1024
        ),
    )(*operands)
    forces, energies = pl.pallas_call(
        settle,
        out_shape=(
            jax.ShapeDtypeStruct(operands[0].shape, F32),
            jax.ShapeDtypeStruct(counts.shape, F32),
        ),
        in_specs=[vmem],
        out_specs=(vmem, vmem),
        compiler_params=pltpu.CompilerParams(vmem_limit_bytes=64 * 1024 * 1024),
    )(back)
    return forces.transpose(0, 2, 1, 3), energies


def solution(mesh):
    per_domain = (
        P("gx", "gy", None, None),
        P("gx", "gy", None),
        P("gx", "gy", None, None),
        P("gx", "gy", None),
        P("gx", "gy", None, None),
        P("gx", "gy", None),
    )
    return jax.shard_map(
        local,
        mesh=mesh,
        in_specs=per_domain + (P(),) * 13,
        out_specs=(P("gx", "gy", None, None), P("gx", "gy", None)),
        check_vma=False,
    )
```
